32 devices in a mesh: grp: 2 (over x), tile: 8 (over z, y), depth: 2 (over core).
Axes of the slice: x: 2, y: 2, z: 4, core: 2. Of those that a mesh axis runs over, the one named last changes fastest.
Arguments:
- tracer_start: float32 [16, 8, 256, 256], P('grp', 'depth', 'tile'), parts along dimension 0, may hold values from -6 to 6
- velocity: float32 [4, 8, 256, 256], P('grp', 'depth', 'tile'), parts along dimension 0, may hold values from -3 to 3
- surface: float32 [512, 256], P(('grp', 'tile')), parts along dimension 0, may hold values from -6 to 6
- mixing: float32 [16, 256, 256], P(('grp', 'depth'), 'tile'), parts along dimension 0, may hold values from 0.05 to 2
- land_mask: int32 [8, 256, 256], P('depth', 'tile'), may hold values 0 or 1
- damping: float32 [256, 256], P('tile'), may hold values from 0.002 to 0.02
- tracer_cot: float32 [16, 8, 256, 256], P('grp', 'depth', 'tile'), parts along dimension 0, may hold values from -6 to 6
- surface_cot: float32 [512, 256], P(('grp', 'tile')), parts along dimension 0, may hold values from -5 to 5
Outputs:
- adj_tracer: float32 [16, 8, 256, 256], P('grp', 'depth', 'tile'), parts along dimension 0
- adj_velocity: float32 [4, 8, 256, 256], P('grp', 'depth', 'tile'), parts along dimension 0
- adj_surface: float32 [512, 256], P(('grp', 'tile')), parts along dimension 0
The draws below stay inside these ranges and needn't reach their ends.
There are 2 independent parts, one for each index of `grp`. The reference program is written for one: setup_inputs(seed, part) draws one part's arguments, and reference() takes and returns one part's arrays. A program takes and returns all parts, laid end to end along the dimension named above; an argument that names none is the same for every part. Nothing has to cross between parts.
All inputs are finite; a program needn't handle non-finite values. No bound on the sum of `land_mask` on one device may be relied on, other than what follows from the above.
Results may differ from the reference program's by a relative error of at most 0.0003.
Values sent between devices are 32-bit elements; how exact they have to be, the bound alone decides.
No kernel may reach another device: no remote copies, remote signals or barrier semaphores. Data moves between devices by JAX's collectives and lax.ppermute only.
A program may use at most 64 MiB of HBM per device.

```python
import math
import jax
import jax.numpy as jnp

NTR = 8
COLS = 256
ITERS = 6
LEVELS = 8
NY = 256


def draw_surface_cot(key, part):
    key = jax.random.fold_in(key, 7)
    return jnp.clip(jax.random.normal(key, (NY, COLS), jnp.float32), -5.0, 5.0)


def with_ends(drawn, own_key, low, high):
    place = [jax.random.randint(jax.random.fold_in(own_key, axis), (), 0, length) for axis, length in enumerate(drawn.shape)]
    main_axis = drawn.shape.index(max(drawn.shape))
    neighbour = place[:main_axis] + [(place[main_axis] + 1) % drawn.shape[main_axis]] + place[main_axis + 1:]
    return drawn.at[tuple(place)].set(low).at[tuple(neighbour)].set(high)


def block_levels(own_key, dims, pieces, low, top_value):
    level = 1.0
    for axis_at, shards_of in pieces:
        draws = jax.random.uniform(jax.random.fold_in(jax.random.fold_in(own_key, 6), axis_at), (shards_of,), jnp.float32, low / len(pieces), top_value / len(pieces))
        level = level * jnp.repeat(jnp.exp(draws), dims[axis_at] // shards_of).reshape((-1,) + (1,) * (len(dims) - 1 - axis_at))
    return level


def gaussian(rng, shape, scale, bound, shards=(), kind=jnp.bfloat16):
    entries = scale * jax.random.normal(rng, shape, jnp.float32)
    if shards:
        entries = entries * block_levels(rng, shape, shards, -0.22, 0.18)
    return jnp.clip(entries, -bound, bound).astype(kind)


def setup_inputs(seed: int = 0, part: int = 0) -> dict:
    keys = jax.random.split(jax.random.key(seed), 9)
    part_keys = jax.random.split(jax.random.fold_in(keys[8], part), 9)
    return {
        "tracer_start": gaussian(part_keys[0], (NTR, LEVELS, NY, COLS), 1.0, 6.0, ((1, 2), (2, 8)), jnp.float32),
        "velocity": gaussian(part_keys[1], (2, LEVELS, NY, COLS), 0.5, 3.0, ((1, 2), (2, 8)), jnp.float32),
        "surface": gaussian(part_keys[2], (NY, COLS), 1.0, 6.0, ((0, 8),), jnp.float32),
        "mixing": jnp.clip(jnp.exp(math.log(2.0) - 3.6888794 * jax.random.uniform(part_keys[3], (LEVELS, NY, COLS), jnp.float32) ** block_levels(part_keys[3], (LEVELS, NY, COLS), ((0, 2), (1, 8)), -0.2, 0.2)), 0.05, 2.0),
        "land_mask": with_ends((jax.random.randint(keys[4], (LEVELS, NY, COLS), 0, 5) < 4).astype(jnp.int32), jax.random.fold_in(keys[4], 1), 0, 1),
        "damping": jnp.clip(jnp.exp(math.log(0.02) - 2.30258502 * jax.random.uniform(keys[5], (NY, COLS), jnp.float32) ** block_levels(keys[5], (NY, COLS), ((0, 8),), -0.2, 0.2)), 0.002, 0.02),
        "tracer_cot": gaussian(part_keys[6], (NTR, LEVELS, NY, COLS), 1.0, 6.0, ((1, 2), (2, 8)), jnp.float32),
        "surface_cot": draw_surface_cot(jax.random.fold_in(jax.random.fold_in(keys[8], part), 71), part),
    }


ADVECT = 0.25
DIFFUSE = 0.1
GRAVITY = 0.5


def next_col(field):
    return jnp.concatenate([field[..., 1:], jnp.zeros_like(field[..., :1])], axis=-1)


def prev_col(field):
    return jnp.concatenate([jnp.zeros_like(field[..., :1]), field[..., :-1]], axis=-1)


def next_row(field):
    return jnp.concatenate([field[..., 1:, :], jnp.zeros_like(field[..., :1, :])], axis=-2)


def prev_row(field):
    return jnp.concatenate([jnp.zeros_like(field[..., :1, :]), field[..., :-1, :]], axis=-2)


def thomas(values, coupling):
    count = coupling.shape[0]
    ratios = []
    partial_value = []
    for level in range(count):
        if level == 0:
            divisor = 1.0 + coupling[0]
            carried = values[..., 0, :, :] / divisor
        else:
            upper_link = coupling[level - 1]
            divisor = 1.0 + coupling[level] + upper_link - upper_link * ratios[level - 1]
            carried = (values[..., level, :, :] + upper_link * partial_value[level - 1]) / divisor
        ratios.append(coupling[level] / divisor)
        partial_value.append(carried)
    solved = [None] * count
    solved[count - 1] = partial_value[count - 1]
    for level in range(count - 2, -1, -1):
        solved[level] = partial_value[level] + ratios[level] * solved[level + 1]
    return jnp.stack(solved, axis=-3)


def surface_op(field, damping):
    beside_all = next_row(field) + prev_row(field) + next_col(field) + prev_col(field)
    return (4.0 + damping) * field - beside_all


def reference(tracer_start, velocity, surface, mixing, land_mask, damping, tracer_cot, surface_cot):
    level_ids = jnp.arange(LEVELS, dtype=jnp.int32)[:, None, None]
    coupling = jnp.where(level_ids < LEVELS - 1, mixing, jnp.float32(0.0))
    settled = thomas(tracer_start, coupling)
    weighted = land_mask.astype(jnp.float32)[None] * tracer_cot
    along_x = next_col(weighted) - prev_col(weighted)
    along_y = next_row(weighted) - prev_row(weighted)
    spread = next_row(weighted) + prev_row(weighted) + next_col(weighted) + prev_col(weighted) - 4.0 * weighted
    u_eff = velocity[0] - GRAVITY * (next_col(surface) - prev_col(surface))
    v_eff = velocity[1] - GRAVITY * (next_row(surface) - prev_row(surface))
    adj_settled = weighted + ADVECT * (u_eff * along_x + v_eff * along_y) + DIFFUSE * spread
    flux_x = ADVECT * jnp.sum(settled * along_x, axis=0)
    flux_y = ADVECT * jnp.sum(settled * along_y, axis=0)
    adj_tracer = thomas(adj_settled, coupling)
    col_x = jnp.sum(flux_x, axis=0)
    col_y = jnp.sum(flux_y, axis=0)
    source = surface_cot + GRAVITY * (next_col(col_x) - prev_col(col_x) + next_row(col_y) - prev_row(col_y))
    solution = jnp.zeros_like(source)
    residual = source
    direction = source
    norm_now = jnp.sum(residual * residual)
    for turn in range(ITERS):
        image = surface_op(direction, damping)
        alpha = norm_now / jnp.sum(direction * image)
        solution = solution + alpha * direction
        residual = residual - alpha * image
        norm_next = jnp.sum(residual * residual)
        direction = residual + (norm_next / norm_now) * direction
        norm_now = norm_next
    adj_velocity = jnp.stack([flux_x + ADVECT * (next_col(solution) - prev_col(solution)),
                              flux_y + ADVECT * (next_row(solution) - prev_row(solution))])
    return adj_tracer, adj_velocity, solution
```

```python
import functools

import jax
import jax.numpy as jnp
from jax import lax
from jax.experimental import pallas as pl
from jax.experimental.pallas import tpu as pltpu
from jax.sharding import PartitionSpec as P

ITERS = 6
ADVECT = 0.25
DIFFUSE = 0.1
GRAVITY = 0.5

F32 = jnp.float32
VMEM = pl.BlockSpec(memory_space=pltpu.VMEM)


def call(kernel, outs, args, scratch=(), flops=2_000_000):
    nbytes = sum(a.size * 4 for a in args) + sum(4 * functools.reduce(lambda p, q: p * q, s) for s in outs)
    return pl.pallas_call(
        kernel,
        out_shape=[jax.ShapeDtypeStruct(s, F32) for s in outs],
        in_specs=[VMEM] * len(args),
        out_specs=[VMEM] * len(outs),
        scratch_shapes=list(scratch),
        cost_estimate=pl.CostEstimate(flops=flops, bytes_accessed=nbytes, transcendentals=0),
        compiler_params=pltpu.CompilerParams(vmem_limit_bytes=40 * 1024 * 1024),
    )(*args)


def lane_shifts(f):
    lane = lax.broadcasted_iota(jnp.int32, f.shape, f.ndim - 1)
    cols = f.shape[-1]
    after = jnp.where(lane == cols - 1, 0.0, pltpu.roll(f, cols - 1, f.ndim - 1))
    before = jnp.where(lane == 0, 0.0, pltpu.roll(f, 1, f.ndim - 1))
    return after, before


def row_shifts(f, low, high):
    row = lax.broadcasted_iota(jnp.int32, f.shape, 0)
    rows = f.shape[0]
    after = jnp.where(row == rows - 1, high, pltpu.roll(f, rows - 1, 0))
    before = jnp.where(row == 0, low, pltpu.roll(f, 1, 0))
    return after, before


def chain(mix_ref, depth):
    levels = mix_ref.shape[0]
    links = [mix_ref[j + depth * (levels - 2 - 2 * j)] for j in range(levels - 1)]
    rest = jnp.ones_like(links[0])
    inverse, ratio = [], []
    for link in links:
        inv = 1.0 / (rest + link)
        inverse.append(inv)
        ratio.append(link * inv)
        rest = 1.0 + link * (rest * inv)
    return inverse, ratio, rest


def level(j, depth, levels):
    return j + depth * (levels - 1 - 2 * j)


def meet(rest, other_rest, own_mix, other_mix, depth):
    link = jnp.where(depth == 0, own_mix, other_mix)
    det = rest * other_rest + link * (rest + other_rest)
    inv = 1.0 / det
    return (other_rest + link) * inv, link * inv


def start_kernel(tracer, mix, cot, mask, surface, face, edge_a, edge_b):
    tracers, levels, rows, _ = tracer.shape
    depth = lax.axis_index("depth")
    odd = lax.rem(lax.axis_index("tile"), 2) == 1
    _, ratio, rest = chain(mix, depth)
    for tr in range(tracers):
        num = tracer[tr, level(0, depth, levels)]
        for j in range(1, levels):
            num = tracer[tr, level(j, depth, levels)] + ratio[j - 1] * num
        face[tr] = num
    face[tracers] = rest
    face[tracers + 1] = mix[levels - 1]
    for lev in range(levels):
        first_mask = mask[lev, 0:1].astype(F32)
        last_mask = mask[lev, rows - 1 : rows].astype(F32)
        for tr in range(tracers):
            first = cot[tr, lev, 0:1] * first_mask
            last = cot[tr, lev, rows - 1 : rows] * last_mask
            at = tr * levels + lev
            edge_a[at : at + 1] = jnp.where(odd, first, last)
            edge_b[at : at + 1] = jnp.where(odd, last, first)
    at = tracers * levels
    edge_a[at : at + 1] = jnp.where(odd, surface[0:1], surface[rows - 1 : rows])
    edge_b[at : at + 1] = jnp.where(odd, surface[rows - 1 : rows], surface[0:1])


def flux_kernel(tracer, mix, cot, mask, face, other, edge_a, edge_b, surface_cot, damping, flux, send):
    tracers, levels, rows, cols = tracer.shape
    depth = lax.axis_index("depth")
    odd = lax.rem(lax.axis_index("tile"), 2) == 1
    inverse, ratio, rest = chain(mix, depth)
    own_w, other_w = meet(rest, other[tracers], mix[levels - 1], other[tracers + 1], depth)
    col_x = jnp.zeros((rows, cols), F32)
    col_y = jnp.zeros((rows, cols), F32)
    flux[...] = jnp.zeros_like(flux)
    for tr in range(tracers):
        nums = [tracer[tr, level(0, depth, levels)]]
        for j in range(1, levels):
            nums.append(tracer[tr, level(j, depth, levels)] + ratio[j - 1] * nums[-1])
        value = own_w * nums[-1] + other_w * other[tr]
        for j in range(levels - 1, -1, -1):
            lev = level(j, depth, levels)
            if j < levels - 1:
                value = inverse[j] * nums[j] + ratio[j] * value
            weighted = cot[tr, lev] * mask[lev].astype(F32)
            at = tr * levels + lev
            row_a, row_b = edge_a[pl.ds(at, 1)], edge_b[pl.ds(at, 1)]
            low, high = jnp.where(odd, row_a, row_b), jnp.where(odd, row_b, row_a)
            right, left = lane_shifts(weighted)
            down, up = row_shifts(weighted, low, high)
            flux[0, lev] += ADVECT * (value * (right - left))
            flux[1, lev] += ADVECT * (value * (down - up))
    for lev in range(levels):
        col_x += flux[0, lev]
        col_y += flux[1, lev]
    right, left = lane_shifts(col_x)
    down, up = row_shifts(col_y, 0.0, 0.0)
    top = depth == 0
    source = GRAVITY * (right - left + down - up)
    send[0:rows] = source + jnp.where(top, surface_cot[...], 0.0)
    send[rows : rows + 8] = jnp.zeros((8, cols), F32)
    send[rows : rows + 1] = col_y[0:1]
    send[rows + 1 : rows + 2] = col_y[rows - 1 : rows]
    send[rows + 8 : 2 * rows + 8] = jnp.where(top, damping[...], 0.0)


def adjoint_kernel(mix, cot, mask, velocity, surface, edge_a, edge_b, nums):
    tracers, levels, rows, cols = cot.shape
    depth = lax.axis_index("depth")
    odd = lax.rem(lax.axis_index("tile"), 2) == 1
    _, ratio, _ = chain(mix, depth)
    at = tracers * levels
    row_a, row_b = edge_a[at : at + 1], edge_b[at : at + 1]
    low, high = jnp.where(odd, row_a, row_b), jnp.where(odd, row_b, row_a)
    right, left = lane_shifts(surface[...])
    down, up = row_shifts(surface[...], low, high)
    slope_x, slope_y = GRAVITY * (right - left), GRAVITY * (down - up)
    for j in range(levels):
        lev = level(j, depth, levels)
        u_eff = ADVECT * (velocity[0, lev] - slope_x)
        v_eff = ADVECT * (velocity[1, lev] - slope_y)
        wet = mask[lev].astype(F32)
        for tr in range(tracers):
            weighted = cot[tr, lev] * wet
            at = tr * levels + lev
            row_a, row_b = edge_a[pl.ds(at, 1)], edge_b[pl.ds(at, 1)]
            low, high = jnp.where(odd, row_a, row_b), jnp.where(odd, row_b, row_a)
            right, left = lane_shifts(weighted)
            down, up = row_shifts(weighted, low, high)
            out = (
                weighted
                + (u_eff * (right - left) + v_eff * (down - up))
                + DIFFUSE * (down + up + right + left - 4.0 * weighted)
            )
            if j > 0:
                out = out + ratio[j - 1] * nums[j - 1, tr]
            nums[j, tr] = out


def finish_kernel(mix, nums, face, other, other_nums, adj_tracer):
    tracers, levels, rows, cols = adj_tracer.shape
    depth = lax.axis_index("depth")
    inverse, ratio, rest = chain(mix, depth)
    own_w, other_w = meet(rest, other[tracers], mix[levels - 1], other[tracers + 1], depth)
    for tr in range(tracers):
        value = own_w * nums[levels - 1, tr] + other_w * other_nums[tr]
        adj_tracer[tr, level(levels - 1, depth, levels)] = value
        for j in range(levels - 2, -1, -1):
            value = inverse[j] * nums[j, tr] + ratio[j] * value
            adj_tracer[tr, level(j, depth, levels)] = value


def solve_kernel(tiles, partners, flux, own, *refs):
    steps = len(partners)
    got, swapped = refs[:steps], refs[steps : 2 * steps]
    adj_velocity, adj_surface, src, damp, edges, direc, image, sol = refs[2 * steps :]
    levels, rows, cols = flux.shape[1:]
    me = lax.axis_index("tile")
    depth = lax.axis_index("depth")

    edges[0:8] = jnp.zeros((8, cols), F32)
    edges[8 * (tiles + 1) : 8 * (tiles + 2)] = jnp.zeros((8, cols), F32)

    def place(ref, tile):
        at = pl.multiple_of(tile * rows, rows)
        src[pl.ds(at, rows)] = ref[0:rows]
        damp[pl.ds(at, rows)] = 4.0 + ref[rows + 8 : 2 * rows + 8]
        edges[pl.ds(pl.multiple_of((tile + 1) * 8, 8), 8)] = ref[rows : rows + 8]

    place(own, me)
    for step, (for_top, for_bottom) in enumerate(partners):
        place(got[step], partner(me, jnp.where(depth == 0, for_top, for_bottom), tiles))
        place(swapped[step], partner(me, jnp.where(depth == 0, for_bottom, for_top), tiles))

    pad = 8
    total = jnp.zeros((rows, cols), F32)
    direc[0:pad] = jnp.zeros((pad, cols), F32)
    direc[pad + tiles * rows : 2 * pad + tiles * rows] = jnp.zeros((pad, cols), F32)
    row = lax.broadcasted_iota(jnp.int32, (rows, cols), 0)
    for t in range(tiles):
        above = edges[8 * t + 1 : 8 * t + 2]
        below = edges[8 * (t + 2) : 8 * (t + 2) + 1]
        block = src[t * rows : (t + 1) * rows]
        block = block + GRAVITY * (jnp.where(row == rows - 1, below, 0.0) - jnp.where(row == 0, above, 0.0))
        src[t * rows : (t + 1) * rows] = block
        direc[pad + t * rows : pad + (t + 1) * rows] = block
        total += block * block
    norm = jnp.sum(total, keepdims=True)
    sol[...] = jnp.zeros_like(sol)
    mine = pl.ds(pl.multiple_of(me * rows, 8), rows + 2 * pad)

    def advance(turn, norm):
        total = jnp.zeros((rows, cols), F32)
        for t in range(tiles):
            at = pad + t * rows
            d = direc[at : at + rows]
            right, left = lane_shifts(d)
            beside = direc[at + 1 : at + rows + 1] + direc[at - 1 : at + rows - 1] + right + left
            im = damp[t * rows : (t + 1) * rows] * d - beside
            image[t * rows : (t + 1) * rows] = im
            total += d * im
        alpha = norm / jnp.sum(total, keepdims=True)
        sol[...] += alpha * direc[mine]
        total = jnp.zeros((rows, cols), F32)
        for t in range(tiles):
            part = slice(t * rows, (t + 1) * rows)
            r = src[part] - alpha * image[part]
            src[part] = r
            total += r * r
        fresh = jnp.sum(total, keepdims=True)
        beta = fresh / norm
        for t in range(tiles):
            at = pad + t * rows
            direc[at : at + rows] = src[t * rows : (t + 1) * rows] + beta * direc[at : at + rows]
        return fresh

    lax.fori_loop(0, ITERS, advance, norm)

    x = sol[pad : pad + rows]
    adj_surface[...] = x
    right, left = lane_shifts(x)
    slope_x = ADVECT * (right - left)
    slope_y = ADVECT * (sol[pad + 1 : pad + rows + 1] - sol[pad - 1 : pad + rows - 1])
    for lev in range(levels):
        adj_velocity[0, lev] = flux[0, lev] + slope_x
        adj_velocity[1, lev] = flux[1, lev] + slope_y


def partner(tile, offset, tiles):
    if tiles & (tiles - 1) == 0:
        return tile ^ offset
    return (offset + tiles - tile) % tiles


def partner_offsets(tiles):
    if tiles & (tiles - 1) == 0:
        others = list(range(1, tiles))
    else:
        others = list(range(tiles))
    half = (len(others) + 1) // 2
    top, bottom = others[:half], others[half:]
    if len(bottom) < half:
        bottom = bottom + [top[-1]]
    return list(zip(top, bottom))


def body(tracer_start, velocity, surface, mixing, land_mask, damping, tracer_cot, surface_cot):
    tracers, levels, rows, cols = tracer_start.shape
    tiles = lax.axis_size("tile")
    swap = [(0, 1), (1, 0)]
    plane = (rows, cols)
    edge = (tracers * levels + 1, cols)
    face, edge_a, edge_b = call(
        start_kernel,
        [(tracers + 2,) + plane, edge, edge],
        [tracer_start, mixing, tracer_cot, land_mask, surface],
    )
    pairs_a = [(i, i + 1) for i in range(0, tiles - 1, 2)]
    pairs_b = [(i, i + 1) for i in range(1, tiles - 1, 2)]
    other = lax.ppermute(face, "depth", swap)
    edge_a = lax.ppermute(edge_a, "tile", pairs_a + [(b, a) for a, b in pairs_a])
    edge_b = lax.ppermute(edge_b, "tile", pairs_b + [(b, a) for a, b in pairs_b])
    flux, part = call(
        flux_kernel,
        [(2, levels) + plane, (2 * rows + 8, cols)],
        [tracer_start, mixing, tracer_cot, land_mask, face, other, edge_a, edge_b, surface_cot, damping],
    )
    own = part + lax.ppermute(part, "depth", swap)

    partners = partner_offsets(tiles)
    got = []
    for for_top, for_bottom in partners:
        pairs = [(2 * partner(t, for_top, tiles), 2 * t) for t in range(tiles)]
        pairs += [(2 * partner(t, for_bottom, tiles) + 1, 2 * t + 1) for t in range(tiles)]
        got.append(lax.ppermute(own, ("tile", "depth"), pairs))
    swapped = [lax.ppermute(block, "depth", swap) for block in got]

    (nums,) = call(
        adjoint_kernel,
        [(levels, tracers) + plane],
        [mixing, tracer_cot, land_mask, velocity, surface, edge_a, edge_b],
        flops=20_000_000,
    )
    other_nums = lax.ppermute(nums[levels - 1], "depth", swap)
    (adj_tracer,) = call(
        finish_kernel,
        [(tracers, levels) + plane],
        [mixing, nums, face, other, other_nums],
    )
    height = tiles * rows
    adj_velocity, adj_surface = call(
        functools.partial(solve_kernel, tiles, partners),
        [(2, levels) + plane, plane],
        [flux, own] + got + swapped,
        scratch=[
            pltpu.VMEM((height, cols), F32),
            pltpu.VMEM((height, cols), F32),
            pltpu.VMEM((8 * (tiles + 2), cols), F32),
            pltpu.VMEM((height + 16, cols), F32),
            pltpu.VMEM((height, cols), F32),
            pltpu.VMEM((rows + 16, cols), F32),
        ],
    )
    return adj_tracer, adj_velocity, adj_surface


def solution(mesh):
    return jax.shard_map(
        body,
        mesh=mesh,
        in_specs=(
            P("grp", "depth", "tile", None),
            P("grp", "depth", "tile", None),
            P(("grp", "tile"), None),
            P(("grp", "depth"), "tile", None),
            P("depth", "tile", None),
            P("tile", None),
            P("grp", "depth", "tile", None),
            P(("grp", "tile"), None),
        ),
        out_specs=(
            P("grp", "depth", "tile", None),
            P("grp", "depth", "tile", None),
            P(("grp", "tile"), None),
        ),
        check_vma=False,
    )
```

```python
import functools

import jax
import jax.numpy as jnp
from jax import lax
from jax.experimental import pallas as pl
from jax.experimental.pallas import tpu as pltpu
from jax.sharding import PartitionSpec as P

ITERS = 6
ADVECT = 0.25
DIFFUSE = 0.1
GRAVITY = 0.5

F32 = jnp.float32
VMEM = pl.BlockSpec(memory_space=pltpu.VMEM)
HBM = pl.BlockSpec(memory_space=pltpu.HBM)


def call(kernel, outs, args, scratch=(), flops=2_000_000, hbm_in=(), hbm_out=()):
    nbytes = sum(a.size * 4 for a in args) + sum(4 * functools.reduce(lambda p, q: p * q, s) for s in outs)
    return pl.pallas_call(
        kernel,
        out_shape=[jax.ShapeDtypeStruct(s, F32) for s in outs],
        in_specs=[HBM if i in hbm_in else VMEM for i in range(len(args))],
        out_specs=[HBM if i in hbm_out else VMEM for i in range(len(outs))],
        scratch_shapes=list(scratch),
        cost_estimate=pl.CostEstimate(flops=flops, bytes_accessed=nbytes, transcendentals=0),
        compiler_params=pltpu.CompilerParams(vmem_limit_bytes=40 * 1024 * 1024),
    )(*args)


def lane_shifts(f):
    lane = lax.broadcasted_iota(jnp.int32, f.shape, f.ndim - 1)
    cols = f.shape[-1]
    after = jnp.where(lane == cols - 1, 0.0, pltpu.roll(f, cols - 1, f.ndim - 1))
    before = jnp.where(lane == 0, 0.0, pltpu.roll(f, 1, f.ndim - 1))
    return after, before


def row_shifts(f, low, high):
    row = lax.broadcasted_iota(jnp.int32, f.shape, 0)
    rows = f.shape[0]
    after = jnp.where(row == rows - 1, high, pltpu.roll(f, rows - 1, 0))
    before = jnp.where(row == 0, low, pltpu.roll(f, 1, 0))
    return after, before


def chain(mix_ref, depth):
    levels = mix_ref.shape[0]
    links = [mix_ref[j + depth * (levels - 2 - 2 * j)] for j in range(levels - 1)]
    rest = jnp.ones_like(links[0])
    inverse, ratio = [], []
    for link in links:
        inv = 1.0 / (rest + link)
        inverse.append(inv)
        ratio.append(link * inv)
        rest = 1.0 + link * (rest * inv)
    return inverse, ratio, rest


def level(j, depth, levels):
    return j + depth * (levels - 1 - 2 * j)


def meet(rest, other_rest, own_mix, other_mix, depth):
    link = jnp.where(depth == 0, own_mix, other_mix)
    det = rest * other_rest + link * (rest + other_rest)
    inv = 1.0 / det
    return (other_rest + link) * inv, link * inv


def start_kernel(tracer_in, mix_in, cot_in, mask_in, surface_in, tracer, mix, weighted, surface, face, edge_a, edge_b, cot, mask, sems):
    tracers, levels, rows, _ = tracer.shape
    depth = lax.axis_index("depth")
    odd = lax.rem(lax.axis_index("tile"), 2) == 1
    moves = [(mix_in, mix), (tracer_in, tracer), (surface_in, surface), (mask_in, mask), (cot_in, cot)]
    copies = [pltpu.make_async_copy(src, dst, sems.at[i]) for i, (src, dst) in enumerate(moves)]
    for copy in copies:
        copy.start()
    copies[0].wait()
    copies[1].wait()
    _, ratio, rest = chain(mix, depth)
    for tr in range(tracers):
        num = tracer[tr, level(0, depth, levels)]
        for j in range(1, levels):
            num = tracer[tr, level(j, depth, levels)] + ratio[j - 1] * num
        face[tr] = num
    face[tracers] = rest
    face[tracers + 1] = mix[levels - 1]
    for copy in copies[2:]:
        copy.wait()
    for lev in range(levels):
        wet = mask[lev].astype(F32)
        for tr in range(tracers):
            block = cot[tr, lev] * wet
            weighted[tr, lev] = block
            first, last = block[0:1], block[rows - 1 : rows]
            at = tr * levels + lev
            edge_a[at : at + 1] = jnp.where(odd, first, last)
            edge_b[at : at + 1] = jnp.where(odd, last, first)
    at = tracers * levels
    edge_a[at : at + 8] = jnp.zeros_like(edge_a[at : at + 8])
    edge_b[at : at + 8] = jnp.zeros_like(edge_b[at : at + 8])
    edge_a[at : at + 1] = jnp.where(odd, surface[0:1], surface[rows - 1 : rows])
    edge_b[at : at + 1] = jnp.where(odd, surface[rows - 1 : rows], surface[0:1])


def flux_kernel(tracer, mix, weighted, face, other, flux, firsts, lasts):
    tracers, levels, rows, cols = tracer.shape
    depth = lax.axis_index("depth")
    inverse, ratio, rest = chain(mix, depth)
    own_w, other_w = meet(rest, other[tracers], mix[levels - 1], other[tracers + 1], depth)
    flux[...] = jnp.zeros_like(flux)
    for tr in range(tracers):
        nums = [tracer[tr, level(0, depth, levels)]]
        for j in range(1, levels):
            nums.append(tracer[tr, level(j, depth, levels)] + ratio[j - 1] * nums[-1])
        value = own_w * nums[-1] + other_w * other[tr]
        for j in range(levels - 1, -1, -1):
            lev = level(j, depth, levels)
            if j < levels - 1:
                value = inverse[j] * nums[j] + ratio[j] * value
            block = weighted[tr, lev]
            right, left = lane_shifts(block)
            down, up = row_shifts(block, 0.0, 0.0)
            flux[0, lev] += ADVECT * (value * (right - left))
            flux[1, lev] += ADVECT * (value * (down - up))
            at = tr * levels + lev
            firsts[pl.ds(at, 1)] = value[0:1]
            lasts[pl.ds(at, 1)] = value[rows - 1 : rows]


def column_kernel(flux_in, firsts, lasts, edge_a, edge_b, surface_cot, damping, flux, send):
    levels, rows, cols = flux.shape[1:]
    planes = firsts.shape[0]
    depth = lax.axis_index("depth")
    odd = lax.rem(lax.axis_index("tile"), 2) == 1
    row_a, row_b = edge_a[0:planes], edge_b[0:planes]
    low = ADVECT * (firsts[...] * jnp.where(odd, row_a, row_b))
    high = ADVECT * (lasts[...] * jnp.where(odd, row_b, row_a))
    row = lax.broadcasted_iota(jnp.int32, (rows, cols), 0)
    kind = lax.broadcasted_iota(jnp.int32, (8, cols), 0)
    def by_level(terms):
        return sum(terms[8 * i : 8 * (i + 1)] for i in range(planes // 8))

    low, high = by_level(low), by_level(high)
    col_x = jnp.zeros((rows, cols), F32)
    col_y = jnp.zeros((rows, cols), F32)
    for lev in range(levels):
        at_level = lax.rem(kind, levels) == lev
        minus = jnp.sum(jnp.where(at_level, low, 0.0), axis=0, keepdims=True)
        plus = jnp.sum(jnp.where(at_level, high, 0.0), axis=0, keepdims=True)
        flux_x = flux_in[0, lev]
        flux_y = flux_in[1, lev] + (jnp.where(row == rows - 1, plus, 0.0) - jnp.where(row == 0, minus, 0.0))
        flux[0, lev] = flux_x
        flux[1, lev] = flux_y
        col_x += flux_x
        col_y += flux_y
    right, left = lane_shifts(col_x)
    down, up = row_shifts(col_y, 0.0, 0.0)
    top = depth == 0
    source = GRAVITY * (right - left + down - up)
    send[0:rows] = source + jnp.where(top, surface_cot[...], 0.0)
    send[rows : rows + 8] = jnp.where(kind == 0, col_y[0:1], jnp.where(kind == 1, col_y[rows - 1 : rows], 0.0))
    send[rows + 8 : 2 * rows + 8] = jnp.where(top, damping[...], 0.0)


def adjoint_kernel(mix, weighted_in, velocity, surface, edge_a, edge_b, after, nums, last):
    tracers, levels, rows, cols = weighted_in.shape
    depth = lax.axis_index("depth")
    odd = lax.rem(lax.axis_index("tile"), 2) == 1
    _, ratio, _ = chain(mix, depth)
    at = tracers * levels
    row_a, row_b = edge_a[at : at + 1], edge_b[at : at + 1]
    low, high = jnp.where(odd, row_a, row_b), jnp.where(odd, row_b, row_a)
    right, left = lane_shifts(surface[...])
    down, up = row_shifts(surface[...], low, high)
    slope_x, slope_y = GRAVITY * (right - left), GRAVITY * (down - up)
    for j in range(levels):
        lev = level(j, depth, levels)
        u_eff = ADVECT * (velocity[0, lev] - slope_x)
        v_eff = ADVECT * (velocity[1, lev] - slope_y)
        for tr in range(tracers):
            weighted = weighted_in[tr, lev]
            at = tr * levels + lev
            row_a, row_b = edge_a[pl.ds(at, 1)], edge_b[pl.ds(at, 1)]
            low, high = jnp.where(odd, row_a, row_b), jnp.where(odd, row_b, row_a)
            right, left = lane_shifts(weighted)
            down, up = row_shifts(weighted, low, high)
            out = (
                weighted
                + (u_eff * (right - left) + v_eff * (down - up))
                + DIFFUSE * (down + up + right + left - 4.0 * weighted)
            )
            if j > 0:
                out = out + ratio[j - 1] * nums[j - 1, tr]
            if j < levels - 1:
                nums[j, tr] = out
            else:
                last[tr] = out


def solve_kernel(tiles, partners, flux, mix, nums, last, face, other, other_last, own, *refs):
    steps = len(partners)
    got, swapped = refs[:steps], refs[steps : 2 * steps]
    adj_tracer_out, adj_velocity, adj_surface = refs[2 * steps : 2 * steps + 3]
    src, damp, edges, direc, image, sol, adj_tracer, sem = refs[2 * steps + 3 :]
    levels, rows, cols = flux.shape[1:]
    me = lax.axis_index("tile")
    depth = lax.axis_index("depth")

    tracers = last.shape[0]
    inverse, ratio, rest = chain(mix, depth)
    own_w, other_w = meet(rest, other[tracers], mix[levels - 1], other[tracers + 1], depth)
    for tr in range(tracers):
        value = own_w * last[tr] + other_w * other_last[tr]
        adj_tracer[tr, level(levels - 1, depth, levels)] = value
        for j in range(levels - 2, -1, -1):
            value = inverse[j] * nums[j, tr] + ratio[j] * value
            adj_tracer[tr, level(j, depth, levels)] = value
    copy_out = pltpu.make_async_copy(adj_tracer, adj_tracer_out, sem)
    copy_out.start()

    edges[0:8] = jnp.zeros((8, cols), F32)
    edges[8 * (tiles + 1) : 8 * (tiles + 2)] = jnp.zeros((8, cols), F32)

    def place(ref, tile):
        at = pl.multiple_of(tile * rows, rows)
        src[pl.ds(at, rows)] = ref[0:rows]
        damp[pl.ds(at, rows)] = 4.0 + ref[rows + 8 : 2 * rows + 8]
        edges[pl.ds(pl.multiple_of((tile + 1) * 8, 8), 8)] = ref[rows : rows + 8]

    place(own, me)
    for step, (for_top, for_bottom) in enumerate(partners):
        place(got[step], partner(me, jnp.where(depth == 0, for_top, for_bottom), tiles))
        place(swapped[step], partner(me, jnp.where(depth == 0, for_bottom, for_top), tiles))

    pad = 8
    total = jnp.zeros((rows, cols), F32)
    direc[0:pad] = jnp.zeros((pad, cols), F32)
    direc[pad + tiles * rows : 2 * pad + tiles * rows] = jnp.zeros((pad, cols), F32)
    row = lax.broadcasted_iota(jnp.int32, (rows, cols), 0)
    for t in range(tiles):
        above = edges[8 * t + 1 : 8 * t + 2]
        below = edges[8 * (t + 2) : 8 * (t + 2) + 1]
        block = src[t * rows : (t + 1) * rows]
        block = block + GRAVITY * (jnp.where(row == rows - 1, below, 0.0) - jnp.where(row == 0, above, 0.0))
        src[t * rows : (t + 1) * rows] = block
        direc[pad + t * rows : pad + (t + 1) * rows] = block
        total += block * block
    norm = jnp.sum(total, keepdims=True)
    sol[...] = jnp.zeros_like(sol)
    mine = pl.ds(pl.multiple_of(me * rows, 8), rows + 2 * pad)

    def advance(turn, norm):
        total = jnp.zeros((rows, cols), F32)
        for t in range(tiles):
            at = pad + t * rows
            d = direc[at : at + rows]
            right, left = lane_shifts(d)
            beside = direc[at + 1 : at + rows + 1] + direc[at - 1 : at + rows - 1] + right + left
            im = damp[t * rows : (t + 1) * rows] * d - beside
            image[t * rows : (t + 1) * rows] = im
            total += d * im
        alpha = norm / jnp.sum(total, keepdims=True)
        sol[...] += alpha * direc[mine]
        total = jnp.zeros((rows, cols), F32)
        for t in range(tiles):
            part = slice(t * rows, (t + 1) * rows)
            r = src[part] - alpha * image[part]
            src[part] = r
            total += r * r
        fresh = jnp.sum(total, keepdims=True)
        beta = fresh / norm
        for t in range(tiles):
            at = pad + t * rows
            direc[at : at + rows] = src[t * rows : (t + 1) * rows] + beta * direc[at : at + rows]
        return fresh

    lax.fori_loop(0, ITERS, advance, norm)

    x = sol[pad : pad + rows]
    adj_surface[...] = x
    right, left = lane_shifts(x)
    slope_x = ADVECT * (right - left)
    slope_y = ADVECT * (sol[pad + 1 : pad + rows + 1] - sol[pad - 1 : pad + rows - 1])
    for lev in range(levels):
        adj_velocity[0, lev] = flux[0, lev] + slope_x
        adj_velocity[1, lev] = flux[1, lev] + slope_y
    copy_out.wait()


def partner(tile, offset, tiles):
    if tiles & (tiles - 1) == 0:
        return tile ^ offset
    return (offset + tiles - tile) % tiles


def partner_offsets(tiles):
    if tiles & (tiles - 1) == 0:
        others = list(range(1, tiles))
    else:
        others = list(range(tiles))
    if len(others) % 2 == 1:
        others = others[:1] + others
    pairs = [(others[i], others[i + 1]) for i in range(0, len(others), 2)]
    return [pair if i % 2 == 0 else pair[::-1] for i, pair in enumerate(pairs)]


def body(tracer_start, velocity, surface, mixing, land_mask, damping, tracer_cot, surface_cot):
    tracers, levels, rows, cols = tracer_start.shape
    tiles = lax.axis_size("tile")
    swap = [(0, 1), (1, 0)]
    plane = (rows, cols)
    block = (tracers, levels) + plane
    edge = (tracers * levels + 8, cols)
    tracer, mix, weighted, surface_in, face, edge_a, edge_b = call(
        start_kernel,
        [block, (levels,) + plane, block, plane, (tracers + 2,) + plane, edge, edge],
        [tracer_start, mixing, tracer_cot, land_mask, surface],
        scratch=[pltpu.VMEM(block, F32), pltpu.VMEM((levels,) + plane, jnp.int32), pltpu.SemaphoreType.DMA((5,))],
        hbm_in=range(5),
    )
    pairs_a = [(i, i + 1) for i in range(0, tiles - 1, 2)]
    pairs_b = [(i, i + 1) for i in range(1, tiles - 1, 2)]
    other = lax.ppermute(face, "depth", swap)
    edge_b = lax.ppermute(edge_b, "tile", pairs_b + [(b, a) for a, b in pairs_b])
    edge_a = lax.ppermute(edge_a, "tile", pairs_a + [(b, a) for a, b in pairs_a])
    flux, firsts, lasts = call(
        flux_kernel,
        [(2, levels) + plane, (tracers * levels, cols), (tracers * levels, cols)],
        [tracer, mix, weighted, face, other],
    )
    flux, part = call(
        column_kernel,
        [(2, levels) + plane, (2 * rows + 8, cols)],
        [flux, firsts, lasts, edge_a, edge_b, surface_cot, damping],
    )
    own = part + lax.ppermute(part, "depth", swap)

    partners = partner_offsets(tiles)
    got = []
    for for_top, for_bottom in partners:
        pairs = [(2 * partner(t, for_top, tiles), 2 * t) for t in range(tiles)]
        pairs += [(2 * partner(t, for_bottom, tiles) + 1, 2 * t + 1) for t in range(tiles)]
        got.append(lax.ppermute(own, ("tile", "depth"), pairs))
    swapped = [lax.ppermute(piece, "depth", swap) for piece in got]

    nums, last = call(
        adjoint_kernel,
        [(levels - 1, tracers) + plane, (tracers,) + plane],
        [mix, weighted, velocity, surface_in, edge_a, edge_b, own],
    )
    other_last = lax.ppermute(last, "depth", swap)
    height = tiles * rows
    return call(
        functools.partial(solve_kernel, tiles, partners),
        [block, (2, levels) + plane, plane],
        [flux, mix, nums, last, face, other, other_last, own] + got + swapped,
        scratch=[
            pltpu.VMEM((height, cols), F32),
            pltpu.VMEM((height, cols), F32),
            pltpu.VMEM((8 * (tiles + 2), cols), F32),
            pltpu.VMEM((height + 16, cols), F32),
            pltpu.VMEM((height, cols), F32),
            pltpu.VMEM((rows + 16, cols), F32),
            pltpu.VMEM(block, F32),
            pltpu.SemaphoreType.DMA(()),
        ],
        hbm_out=(0,),
    )


def solution(mesh):
    return jax.shard_map(
        body,
        mesh=mesh,
        in_specs=(
            P("grp", "depth", "tile", None),
            P("grp", "depth", "tile", None),
            P(("grp", "tile"), None),
            P(("grp", "depth"), "tile", None),
            P("depth", "tile", None),
            P("tile", None),
            P("grp", "depth", "tile", None),
            P(("grp", "tile"), None),
        ),
        out_specs=(
            P("grp", "depth", "tile", None),
            P("grp", "depth", "tile", None),
            P(("grp", "tile"), None),
        ),
        check_vma=False,
    )
```

```python
import functools

import jax
import jax.numpy as jnp
from jax import lax
from jax.experimental import pallas as pl
from jax.experimental.pallas import tpu as pltpu
from jax.sharding import PartitionSpec as P

ITERS = 6
ADVECT = 0.25
DIFFUSE = 0.1
GRAVITY = 0.5

F32 = jnp.float32
VMEM = pl.BlockSpec(memory_space=pltpu.VMEM)
HBM = pl.BlockSpec(memory_space=pltpu.HBM)


def call(kernel, outs, args, scratch=(), flops=2_000_000, hbm_in=(), hbm_out=(), vmem=40):
    nbytes = sum(a.size * 4 for a in args) + sum(4 * functools.reduce(lambda p, q: p * q, s) for s in outs)
    return pl.pallas_call(
        kernel,
        out_shape=[jax.ShapeDtypeStruct(s, F32) for s in outs],
        in_specs=[HBM if i in hbm_in else VMEM for i in range(len(args))],
        out_specs=[HBM if i in hbm_out else VMEM for i in range(len(outs))],
        scratch_shapes=list(scratch),
        cost_estimate=pl.CostEstimate(flops=flops, bytes_accessed=nbytes, transcendentals=0),
        compiler_params=pltpu.CompilerParams(vmem_limit_bytes=int(vmem * 1024 * 1024)),
    )(*args)


def lane_shifts(f):
    lane = lax.broadcasted_iota(jnp.int32, f.shape, f.ndim - 1)
    cols = f.shape[-1]
    after = jnp.where(lane == cols - 1, 0.0, pltpu.roll(f, cols - 1, f.ndim - 1))
    before = jnp.where(lane == 0, 0.0, pltpu.roll(f, 1, f.ndim - 1))
    return after, before


def row_shifts(f, low, high):
    row = lax.broadcasted_iota(jnp.int32, f.shape, 0)
    rows = f.shape[0]
    after = jnp.where(row == rows - 1, high, pltpu.roll(f, rows - 1, 0))
    before = jnp.where(row == 0, low, pltpu.roll(f, 1, 0))
    return after, before


def chain(mix_ref, depth):
    levels = mix_ref.shape[0]
    links = [mix_ref[j + depth * (levels - 2 - 2 * j)] for j in range(levels - 1)]
    rest = jnp.ones_like(links[0])
    inverse, ratio = [], []
    for link in links:
        inv = 1.0 / (rest + link)
        inverse.append(inv)
        ratio.append(link * inv)
        rest = 1.0 + link * (rest * inv)
    return inverse, ratio, rest


def level(j, depth, levels):
    return j + depth * (levels - 1 - 2 * j)


def meet(rest, other_rest, own_mix, other_mix, depth):
    link = jnp.where(depth == 0, own_mix, other_mix)
    det = rest * other_rest + link * (rest + other_rest)
    inv = 1.0 / det
    return (other_rest + link) * inv, link * inv


def start_kernel(tracer_in, mix_in, cot_in, mask_in, surface_in, face, edge_b, edge_a, tracer, mix, surface, cot, mask, sems):
    tracers, levels, rows, _ = tracer.shape
    depth = lax.axis_index("depth")
    odd = lax.rem(lax.axis_index("tile"), 2) == 1
    moves = [(mix_in, mix), (tracer_in, tracer), (surface_in, surface), (mask_in, mask)]
    moves += [(cot_in.at[:, :, 0:8], cot.at[0]), (cot_in.at[:, :, rows - 8 : rows], cot.at[1])]
    copies = [pltpu.make_async_copy(src, dst, sems.at[i]) for i, (src, dst) in enumerate(moves)]
    for copy in copies:
        copy.start()
    copies[0].wait()
    copies[1].wait()
    _, ratio, rest = chain(mix, depth)
    for tr in range(tracers):
        num = tracer[tr, level(0, depth, levels)]
        for j in range(1, levels):
            num = tracer[tr, level(j, depth, levels)] + ratio[j - 1] * num
        face[tr] = num
    face[tracers] = rest
    face[tracers + 1] = mix[levels - 1]
    for copy in copies[2:]:
        copy.wait()
    for lev in range(levels):
        first_wet = mask[lev, 0:1].astype(F32)
        last_wet = mask[lev, rows - 1 : rows].astype(F32)
        for tr in range(tracers):
            first = cot[0, tr, lev, 0:1] * first_wet
            last = cot[1, tr, lev, 7:8] * last_wet
            at = lev * tracers + tr
            edge_a[at : at + 1] = jnp.where(odd, first, last)
            edge_b[at : at + 1] = jnp.where(odd, last, first)
    at = tracers * levels
    edge_a[at : at + 8] = jnp.zeros_like(edge_a[at : at + 8])
    edge_b[at : at + 8] = jnp.zeros_like(edge_b[at : at + 8])
    edge_a[at : at + 1] = jnp.where(odd, surface[0:1], surface[rows - 1 : rows])
    edge_b[at : at + 1] = jnp.where(odd, surface[rows - 1 : rows], surface[0:1])


def interior_kernel(tracer, mix, cot, mask, velocity, surface, other, flux, nums, last, packed, lines, speed):
    tracers, levels, rows, cols = tracer.shape
    depth = lax.axis_index("depth")
    inverse, ratio, rest = chain(mix, depth)
    own_w, other_w = meet(rest, other[tracers], mix[levels - 1], other[tracers + 1], depth)
    right, left = lane_shifts(surface[...])
    down, up = row_shifts(surface[...], 0.0, 0.0)
    for lev in range(levels):
        speed[0, lev] = ADVECT * (velocity[0, lev] - GRAVITY * (right - left))
        along = ADVECT * (velocity[1, lev] - GRAVITY * (down - up))
        speed[1, lev] = along
        lines[lev : lev + 1] = along[0:1]
        lines[levels + lev : levels + lev + 1] = along[rows - 1 : rows]
    lines[2 * levels : 4 * levels] = jnp.zeros((2 * levels, cols), F32)
    for j in range(levels - 1):
        at = 2 * levels + j
        lines[at : at + 1] = ratio[j][0:1]
        lines[at + levels : at + levels + 1] = ratio[j][rows - 1 : rows]
    flux[...] = jnp.zeros_like(flux)
    for tr in range(tracers):
        held = [tracer[tr, level(0, depth, levels)]]
        for j in range(1, levels):
            held.append(tracer[tr, level(j, depth, levels)] + ratio[j - 1] * held[-1])
        value = own_w * held[-1] + other_w * other[tr]
        outs = [None] * levels
        for j in range(levels - 1, -1, -1):
            lev = level(j, depth, levels)
            if j < levels - 1:
                value = inverse[j] * held[j] + ratio[j] * value
            block = cot[tr, lev] * mask[lev].astype(F32)
            right, left = lane_shifts(block)
            down, up = row_shifts(block, 0.0, 0.0)
            across, along = right - left, down - up
            flux[0, lev] += ADVECT * (value * across)
            flux[1, lev] += ADVECT * (value * along)
            outs[j] = (
                block
                + (speed[0, lev] * across + speed[1, lev] * along)
                + DIFFUSE * (down + up + right + left - 4.0 * block)
            )
            at = lev * tracers + tr
            packed[0, pl.ds(at, 1)] = value[0:1]
            packed[1, pl.ds(at, 1)] = value[rows - 1 : rows]
            packed[2, pl.ds(at, 1)] = block[1:2]
            packed[3, pl.ds(at, 1)] = block[rows - 2 : rows - 1]
        num = outs[0]
        for j in range(1, levels):
            nums[j - 1, tr] = num
            num = outs[j] + ratio[j - 1] * num
        last[tr] = num


def column_kernel(flux_in, packed, lines, edge_b, edge_a, surface_cot, damping, flux, delta, send):
    levels, rows, cols = flux.shape[1:]
    tracers = delta.shape[2]
    depth = lax.axis_index("depth")
    odd = lax.rem(lax.axis_index("tile"), 2) == 1
    row = lax.broadcasted_iota(jnp.int32, (rows, cols), 0)
    kind = lax.broadcasted_iota(jnp.int32, (8, cols), 0)

    def halo(at, size):
        from_a, from_b = edge_a[pl.ds(at, size)], edge_b[pl.ds(at, size)]
        return jnp.where(odd, from_a, from_b), jnp.where(odd, from_b, from_a)

    col_x = jnp.zeros((rows, cols), F32)
    col_y = jnp.zeros((rows, cols), F32)
    for lev in range(levels):
        low, high = halo(lev * tracers, tracers)
        at = slice(lev * tracers, (lev + 1) * tracers)
        minus = ADVECT * jnp.sum(packed[0, at] * low, axis=0, keepdims=True)
        plus = ADVECT * jnp.sum(packed[1, at] * high, axis=0, keepdims=True)
        flux_x = flux_in[0, lev]
        flux_y = flux_in[1, lev] + (jnp.where(row == rows - 1, plus, 0.0) - jnp.where(row == 0, minus, 0.0))
        flux[0, lev] = flux_x
        flux[1, lev] = flux_y
        col_x += flux_x
        col_y += flux_y
    right, left = lane_shifts(col_x)
    down, up = row_shifts(col_y, 0.0, 0.0)
    top = depth == 0
    source = GRAVITY * (right - left + down - up)
    send[0:rows] = source + jnp.where(top, surface_cot[...], 0.0)
    send[rows : rows + 8] = jnp.where(kind == 0, col_y[0:1], jnp.where(kind == 1, col_y[rows - 1 : rows], 0.0))
    send[rows + 8 : 2 * rows + 8] = jnp.where(top, damping[...], 0.0)

    low_s, high_s = halo(levels * tracers, 8)
    low_s, high_s = ADVECT * GRAVITY * low_s[0:1], ADVECT * GRAVITY * high_s[0:1]
    for j in range(levels):
        lev = level(j, depth, levels)
        at = pl.multiple_of(lev * tracers, tracers)
        low, high = halo(at, tracers)
        first = low_s * packed[2, pl.ds(at, tracers)] + (DIFFUSE - (lines[pl.ds(lev, 1)] + low_s)) * low
        final = high_s * packed[3, pl.ds(at, tracers)] + (DIFFUSE + (lines[pl.ds(levels + lev, 1)] - high_s)) * high
        if j > 0:
            first = first + lines[2 * levels + j - 1 : 2 * levels + j] * delta[0, j - 1]
            final = final + lines[3 * levels + j - 1 : 3 * levels + j] * delta[1, j - 1]
        delta[0, j] = first
        delta[1, j] = final
    send[2 * rows + 8 : 2 * rows + 8 + tracers] = delta[0, levels - 1]
    send[2 * rows + 8 + tracers : 2 * rows + 8 + 2 * tracers] = delta[1, levels - 1]


def solve_kernel(tiles, partners, flux, mix, nums, last, delta, other, other_last, swept, own, *refs):
    steps = len(partners)
    got, swapped = refs[:steps], refs[steps : 2 * steps]
    adj_tracer_out, adj_velocity, adj_surface = refs[2 * steps : 2 * steps + 3]
    src, damp, edges, direc, image, sol, adj_tracer, sem = refs[2 * steps + 3 :]
    levels, rows, cols = flux.shape[1:]
    me = lax.axis_index("tile")
    depth = lax.axis_index("depth")

    tracers = last.shape[0]
    inverse, ratio, rest = chain(mix, depth)
    own_w, other_w = meet(rest, other[tracers], mix[levels - 1], other[tracers + 1], depth)
    row = lax.broadcasted_iota(jnp.int32, (rows, cols), 0)
    far = 2 * rows + 8

    def with_rows(block, first, final):
        return block + (jnp.where(row == 0, first, 0.0) + jnp.where(row == rows - 1, final, 0.0))

    for tr in range(tracers):
        num = with_rows(last[tr], delta[0, levels - 1, tr : tr + 1], delta[1, levels - 1, tr : tr + 1])
        at = far + tr
        other_num = with_rows(other_last[tr], swept[at : at + 1], swept[at + tracers : at + tracers + 1])
        value = own_w * num + other_w * other_num
        adj_tracer[tr, level(levels - 1, depth, levels)] = value
        for j in range(levels - 2, -1, -1):
            num = with_rows(nums[j, tr], delta[0, j, tr : tr + 1], delta[1, j, tr : tr + 1])
            value = inverse[j] * num + ratio[j] * value
            adj_tracer[tr, level(j, depth, levels)] = value
    copy_out = pltpu.make_async_copy(adj_tracer, adj_tracer_out, sem)
    copy_out.start()

    edges[0:8] = jnp.zeros((8, cols), F32)
    edges[8 * (tiles + 1) : 8 * (tiles + 2)] = jnp.zeros((8, cols), F32)

    def place(ref, tile):
        at = pl.multiple_of(tile * rows, rows)
        src[pl.ds(at, rows)] = ref[0:rows]
        damp[pl.ds(at, rows)] = 4.0 + ref[rows + 8 : 2 * rows + 8]
        edges[pl.ds(pl.multiple_of((tile + 1) * 8, 8), 8)] = ref[rows : rows + 8]

    place(own, me)
    for step, (for_top, for_bottom) in enumerate(partners):
        place(got[step], partner(me, jnp.where(depth == 0, for_top, for_bottom), tiles))
        place(swapped[step], partner(me, jnp.where(depth == 0, for_bottom, for_top), tiles))

    pad = 8
    total = jnp.zeros((rows, cols), F32)
    direc[0:pad] = jnp.zeros((pad, cols), F32)
    direc[pad + tiles * rows : 2 * pad + tiles * rows] = jnp.zeros((pad, cols), F32)
    for t in range(tiles):
        above = edges[8 * t + 1 : 8 * t + 2]
        below = edges[8 * (t + 2) : 8 * (t + 2) + 1]
        block = src[t * rows : (t + 1) * rows]
        block = block + GRAVITY * (jnp.where(row == rows - 1, below, 0.0) - jnp.where(row == 0, above, 0.0))
        src[t * rows : (t + 1) * rows] = block
        direc[pad + t * rows : pad + (t + 1) * rows] = block
        total += block * block
    norm = jnp.sum(total, keepdims=True)
    sol[...] = jnp.zeros_like(sol)
    mine = pl.ds(pl.multiple_of(me * rows, 8), rows + 2 * pad)

    def advance(turn, norm):
        total = jnp.zeros((rows, cols), F32)
        for t in range(tiles):
            at = pad + t * rows
            d = direc[at : at + rows]
            right, left = lane_shifts(d)
            beside = direc[at + 1 : at + rows + 1] + direc[at - 1 : at + rows - 1] + right + left
            im = damp[t * rows : (t + 1) * rows] * d - beside
            image[t * rows : (t + 1) * rows] = im
            total += d * im
        alpha = norm / jnp.sum(total, keepdims=True)
        sol[...] += alpha * direc[mine]
        total = jnp.zeros((rows, cols), F32)
        for t in range(tiles):
            part = slice(t * rows, (t + 1) * rows)
            r = src[part] - alpha * image[part]
            src[part] = r
            total += r * r
        fresh = jnp.sum(total, keepdims=True)
        beta = fresh / norm
        for t in range(tiles):
            at = pad + t * rows
            direc[at : at + rows] = src[t * rows : (t + 1) * rows] + beta * direc[at : at + rows]
        return fresh

    lax.fori_loop(0, ITERS, advance, norm)

    x = sol[pad : pad + rows]
    adj_surface[...] = x
    right, left = lane_shifts(x)
    slope_x = ADVECT * (right - left)
    slope_y = ADVECT * (sol[pad + 1 : pad + rows + 1] - sol[pad - 1 : pad + rows - 1])
    for lev in range(levels):
        adj_velocity[0, lev] = flux[0, lev] + slope_x
        adj_velocity[1, lev] = flux[1, lev] + slope_y
    copy_out.wait()


def partner(tile, offset, tiles):
    if tiles & (tiles - 1) == 0:
        return tile ^ offset
    return (offset + tiles - tile) % tiles


def partner_offsets(tiles):
    if tiles & (tiles - 1) == 0:
        others = list(range(1, tiles))
    else:
        others = list(range(tiles))
    if len(others) % 2 == 1:
        others = others[:1] + others
    pairs = [(others[i], others[i + 1]) for i in range(0, len(others), 2)]
    return [pair if i % 2 == 0 else pair[::-1] for i, pair in enumerate(pairs)]


def body(tracer_start, velocity, surface, mixing, land_mask, damping, tracer_cot, surface_cot):
    tracers, levels, rows, cols = tracer_start.shape
    tiles = lax.axis_size("tile")
    swap = [(0, 1), (1, 0)]
    plane = (rows, cols)
    block = (tracers, levels) + plane
    edge = (tracers * levels + 8, cols)
    face, edge_b, edge_a = call(
        start_kernel,
        [(tracers + 2,) + plane, edge, edge],
        [tracer_start, mixing, tracer_cot, land_mask, surface],
        scratch=[
            pltpu.VMEM(block, F32),
            pltpu.VMEM((levels,) + plane, F32),
            pltpu.VMEM(plane, F32),
            pltpu.VMEM((2, tracers, levels, 8, cols), F32),
            pltpu.VMEM((levels,) + plane, jnp.int32),
            pltpu.SemaphoreType.DMA((6,)),
        ],
        hbm_in=range(5),
        vmem=56,
    )
    pairs_a = [(i, i + 1) for i in range(0, tiles - 1, 2)]
    pairs_b = [(i, i + 1) for i in range(1, tiles - 1, 2)]
    other = lax.ppermute(face, "depth", swap)
    edge_b = lax.ppermute(edge_b, "tile", pairs_b + [(b, a) for a, b in pairs_b])
    edge_a = lax.ppermute(edge_a, "tile", pairs_a + [(b, a) for a, b in pairs_a])
    planes = tracers * levels
    flux, nums, last, packed, lines = call(
        interior_kernel,
        [(2, levels) + plane, (levels - 1, tracers) + plane, (tracers,) + plane, (4, planes, cols), (4 * levels, cols)],
        [tracer_start, mixing, tracer_cot, land_mask, velocity, surface, other],
        scratch=[pltpu.VMEM((2, levels) + plane, F32)],
    )
    other_last = lax.ppermute(last, "depth", swap)
    flux, delta, part = call(
        column_kernel,
        [(2, levels) + plane, (2, levels, tracers, cols), (2 * rows + 8 + 2 * tracers, cols)],
        [flux, packed, lines, edge_b, edge_a, surface_cot, damping],
    )
    swept = lax.ppermute(part, "depth", swap)
    own = part[: 2 * rows + 8] + swept[: 2 * rows + 8]

    partners = partner_offsets(tiles)
    got = []
    for for_top, for_bottom in partners:
        pairs = [(2 * partner(t, for_top, tiles), 2 * t) for t in range(tiles)]
        pairs += [(2 * partner(t, for_bottom, tiles) + 1, 2 * t + 1) for t in range(tiles)]
        got.append(lax.ppermute(own, ("tile", "depth"), pairs))
    swapped = [lax.ppermute(piece, "depth", swap) for piece in got]

    height = tiles * rows
    return call(
        functools.partial(solve_kernel, tiles, partners),
        [block, (2, levels) + plane, plane],
        [flux, mixing, nums, last, delta, other, other_last, swept, own] + got + swapped,
        scratch=[
            pltpu.VMEM((height, cols), F32),
            pltpu.VMEM((height, cols), F32),
            pltpu.VMEM((8 * (tiles + 2), cols), F32),
            pltpu.VMEM((height + 16, cols), F32),
            pltpu.VMEM((height, cols), F32),
            pltpu.VMEM((rows + 16, cols), F32),
            pltpu.VMEM(block, F32),
            pltpu.SemaphoreType.DMA(()),
        ],
        hbm_out=(0,),
    )


def solution(mesh):
    return jax.shard_map(
        body,
        mesh=mesh,
        in_specs=(
            P("grp", "depth", "tile", None),
            P("grp", "depth", "tile", None),
            P(("grp", "tile"), None),
            P(("grp", "depth"), "tile", None),
            P("depth", "tile", None),
            P("tile", None),
            P("grp", "depth", "tile", None),
            P(("grp", "tile"), None),
        ),
        out_specs=(
            P("grp", "depth", "tile", None),
            P("grp", "depth", "tile", None),
            P(("grp", "tile"), None),
        ),
        check_vma=False,
    )
```

```python
import functools

import jax
import jax.numpy as jnp
from jax import lax
from jax.experimental import pallas as pl
from jax.experimental.pallas import tpu as pltpu
from jax.sharding import PartitionSpec as P

ITERS = 6
ADVECT = 0.25
DIFFUSE = 0.1
GRAVITY = 0.5

F32 = jnp.float32
VMEM = pl.BlockSpec(memory_space=pltpu.VMEM)
HBM = pl.BlockSpec(memory_space=pltpu.HBM)


def call(kernel, outs, args, scratch=(), flops=2_000_000, hbm_in=(), hbm_out=(), vmem=40):
    nbytes = sum(a.size * 4 for a in args) + sum(4 * functools.reduce(lambda p, q: p * q, s) for s in outs)
    return pl.pallas_call(
        kernel,
        out_shape=[jax.ShapeDtypeStruct(s, F32) for s in outs],
        in_specs=[HBM if i in hbm_in else VMEM for i in range(len(args))],
        out_specs=[HBM if i in hbm_out else VMEM for i in range(len(outs))],
        scratch_shapes=list(scratch),
        cost_estimate=pl.CostEstimate(flops=flops, bytes_accessed=nbytes, transcendentals=0),
        compiler_params=pltpu.CompilerParams(vmem_limit_bytes=int(vmem * 1024 * 1024)),
    )(*args)


def lane_shifts(f):
    lane = lax.broadcasted_iota(jnp.int32, f.shape, f.ndim - 1)
    cols = f.shape[-1]
    after = jnp.where(lane == cols - 1, 0.0, pltpu.roll(f, cols - 1, f.ndim - 1))
    before = jnp.where(lane == 0, 0.0, pltpu.roll(f, 1, f.ndim - 1))
    return after, before


def row_shifts(f, low, high):
    row = lax.broadcasted_iota(jnp.int32, f.shape, 0)
    rows = f.shape[0]
    after = jnp.where(row == rows - 1, high, pltpu.roll(f, rows - 1, 0))
    before = jnp.where(row == 0, low, pltpu.roll(f, 1, 0))
    return after, before


def chain(mix_ref, depth):
    levels = mix_ref.shape[0]
    links = [mix_ref[j + depth * (levels - 2 - 2 * j)] for j in range(levels - 1)]
    rest = jnp.ones_like(links[0])
    inverse, ratio = [], []
    for link in links:
        inv = 1.0 / (rest + link)
        inverse.append(inv)
        ratio.append(link * inv)
        rest = 1.0 + link * (rest * inv)
    return inverse, ratio, rest


def level(j, depth, levels):
    return j + depth * (levels - 1 - 2 * j)


def meet(rest, other_rest, own_mix, other_mix, depth):
    link = jnp.where(depth == 0, own_mix, other_mix)
    det = rest * other_rest + link * (rest + other_rest)
    inv = 1.0 / det
    return (other_rest + link) * inv, link * inv


def start_kernel(tracer_in, mix_in, cot_in, mask_in, surface_in, face, edge_b, edge_a, tracer, mix, surface, cot, mask, sems):
    tracers, levels, rows, _ = tracer.shape
    depth = lax.axis_index("depth")
    odd = lax.rem(lax.axis_index("tile"), 2) == 1
    moves = [(mix_in, mix), (tracer_in, tracer), (surface_in, surface), (mask_in, mask)]
    moves += [(cot_in.at[:, :, 0:8], cot.at[0]), (cot_in.at[:, :, rows - 8 : rows], cot.at[1])]
    copies = [pltpu.make_async_copy(src, dst, sems.at[i]) for i, (src, dst) in enumerate(moves)]
    for copy in copies:
        copy.start()
    copies[0].wait()
    copies[1].wait()
    _, ratio, rest = chain(mix, depth)
    for tr in range(tracers):
        num = tracer[tr, level(0, depth, levels)]
        for j in range(1, levels):
            num = tracer[tr, level(j, depth, levels)] + ratio[j - 1] * num
        face[tr] = num
    face[tracers] = rest
    face[tracers + 1] = mix[levels - 1]
    for copy in copies[2:]:
        copy.wait()
    for lev in range(levels):
        first_wet = mask[lev, 0:1].astype(F32)
        last_wet = mask[lev, rows - 1 : rows].astype(F32)
        for tr in range(tracers):
            first = cot[0, tr, lev, 0:1] * first_wet
            last = cot[1, tr, lev, 7:8] * last_wet
            at = lev * tracers + tr
            edge_a[at : at + 1] = jnp.where(odd, first, last)
            edge_b[at : at + 1] = jnp.where(odd, last, first)
    at = tracers * levels
    edge_a[at : at + 8] = jnp.zeros_like(edge_a[at : at + 8])
    edge_b[at : at + 8] = jnp.zeros_like(edge_b[at : at + 8])
    edge_a[at : at + 1] = jnp.where(odd, surface[0:1], surface[rows - 1 : rows])
    edge_b[at : at + 1] = jnp.where(odd, surface[rows - 1 : rows], surface[0:1])


def interior_kernel(tracer, mix, cot, mask, velocity, surface, other, flux, nums, last, packed, lines, speed):
    tracers, levels, rows, cols = tracer.shape
    depth = lax.axis_index("depth")
    inverse, ratio, rest = chain(mix, depth)
    own_w, other_w = meet(rest, other[tracers], mix[levels - 1], other[tracers + 1], depth)
    right, left = lane_shifts(surface[...])
    down, up = row_shifts(surface[...], 0.0, 0.0)
    for lev in range(levels):
        speed[0, lev] = ADVECT * (velocity[0, lev] - GRAVITY * (right - left))
        along = ADVECT * (velocity[1, lev] - GRAVITY * (down - up))
        speed[1, lev] = along
        lines[lev : lev + 1] = along[0:1]
        lines[levels + lev : levels + lev + 1] = along[rows - 1 : rows]
    lines[2 * levels : 4 * levels] = jnp.zeros((2 * levels, cols), F32)
    for j in range(levels - 1):
        at = 2 * levels + j
        lines[at : at + 1] = ratio[j][0:1]
        lines[at + levels : at + levels + 1] = ratio[j][rows - 1 : rows]
    flux[...] = jnp.zeros_like(flux)
    for tr in range(tracers):
        held = [tracer[tr, level(0, depth, levels)]]
        for j in range(1, levels):
            held.append(tracer[tr, level(j, depth, levels)] + ratio[j - 1] * held[-1])
        value = own_w * held[-1] + other_w * other[tr]
        outs = [None] * levels
        for j in range(levels - 1, -1, -1):
            lev = level(j, depth, levels)
            if j < levels - 1:
                value = inverse[j] * held[j] + ratio[j] * value
            block = cot[tr, lev] * mask[lev].astype(F32)
            right, left = lane_shifts(block)
            down, up = row_shifts(block, 0.0, 0.0)
            across, along = right - left, down - up
            flux[0, lev] += ADVECT * (value * across)
            flux[1, lev] += ADVECT * (value * along)
            outs[j] = (
                block
                + (speed[0, lev] * across + speed[1, lev] * along)
                + DIFFUSE * (down + up + right + left - 4.0 * block)
            )
            at = lev * tracers + tr
            packed[0, pl.ds(at, 1)] = value[0:1]
            packed[1, pl.ds(at, 1)] = value[rows - 1 : rows]
            packed[2, pl.ds(at, 1)] = block[1:2]
            packed[3, pl.ds(at, 1)] = block[rows - 2 : rows - 1]
        num = outs[0]
        for j in range(1, levels):
            nums[j - 1, tr] = num
            num = outs[j] + ratio[j - 1] * num
        last[tr] = num


def column_kernel(flux_in, packed, lines, edge_b, edge_a, surface_cot, damping, flux, delta, send):
    levels, rows, cols = flux.shape[1:]
    tracers = delta.shape[2]
    depth = lax.axis_index("depth")
    odd = lax.rem(lax.axis_index("tile"), 2) == 1
    row = lax.broadcasted_iota(jnp.int32, (rows, cols), 0)
    kind = lax.broadcasted_iota(jnp.int32, (8, cols), 0)

    def halo(at, size):
        from_a, from_b = edge_a[pl.ds(at, size)], edge_b[pl.ds(at, size)]
        return jnp.where(odd, from_a, from_b), jnp.where(odd, from_b, from_a)

    col_x = jnp.zeros((rows, cols), F32)
    col_y = jnp.zeros((rows, cols), F32)
    for lev in range(levels):
        low, high = halo(lev * tracers, tracers)
        at = slice(lev * tracers, (lev + 1) * tracers)
        minus = ADVECT * jnp.sum(packed[0, at] * low, axis=0, keepdims=True)
        plus = ADVECT * jnp.sum(packed[1, at] * high, axis=0, keepdims=True)
        flux_x = flux_in[0, lev]
        flux_y = flux_in[1, lev] + (jnp.where(row == rows - 1, plus, 0.0) - jnp.where(row == 0, minus, 0.0))
        flux[0, lev] = flux_x
        flux[1, lev] = flux_y
        col_x += flux_x
        col_y += flux_y
    right, left = lane_shifts(col_x)
    down, up = row_shifts(col_y, 0.0, 0.0)
    top = depth == 0
    source = GRAVITY * (right - left + down - up)
    send[0:rows] = source + jnp.where(top, surface_cot[...], 0.0)
    send[rows : rows + 8] = jnp.where(kind == 0, col_y[0:1], jnp.where(kind == 1, col_y[rows - 1 : rows], 0.0))
    send[rows + 8 : 2 * rows + 8] = jnp.where(top, damping[...], 0.0)

    low_s, high_s = halo(levels * tracers, 8)
    low_s, high_s = ADVECT * GRAVITY * low_s[0:1], ADVECT * GRAVITY * high_s[0:1]
    for j in range(levels):
        lev = level(j, depth, levels)
        at = pl.multiple_of(lev * tracers, tracers)
        low, high = halo(at, tracers)
        first = low_s * packed[2, pl.ds(at, tracers)] + (DIFFUSE - (lines[pl.ds(lev, 1)] + low_s)) * low
        final = high_s * packed[3, pl.ds(at, tracers)] + (DIFFUSE + (lines[pl.ds(levels + lev, 1)] - high_s)) * high
        if j > 0:
            first = first + lines[2 * levels + j - 1 : 2 * levels + j] * delta[0, j - 1]
            final = final + lines[3 * levels + j - 1 : 3 * levels + j] * delta[1, j - 1]
        delta[0, j] = first
        delta[1, j] = final
    send[2 * rows + 8 : 2 * rows + 8 + tracers] = delta[0, levels - 1]
    send[2 * rows + 8 + tracers : 2 * rows + 8 + 2 * tracers] = delta[1, levels - 1]


def solve_kernel(tiles, partners, flux, mix, nums, last, delta, other, other_last, swept, own, *refs):
    steps = len(partners)
    got, swapped = refs[:steps], refs[steps : 2 * steps]
    adj_tracer_out, adj_velocity, adj_surface = refs[2 * steps : 2 * steps + 3]
    resid, image, moved, damp, firsts, finals, direc, sol, adj_tracer, sem = refs[2 * steps + 3 :]
    levels, rows, cols = flux.shape[1:]
    me = lax.axis_index("tile")
    depth = lax.axis_index("depth")

    tracers = last.shape[0]
    inverse, ratio, rest = chain(mix, depth)
    own_w, other_w = meet(rest, other[tracers], mix[levels - 1], other[tracers + 1], depth)
    row = lax.broadcasted_iota(jnp.int32, (rows, cols), 0)
    far = 2 * rows + 8

    def with_rows(block, first, final):
        return block + (jnp.where(row == 0, first, 0.0) + jnp.where(row == rows - 1, final, 0.0))

    for tr in range(tracers):
        num = with_rows(last[tr], delta[0, levels - 1, tr : tr + 1], delta[1, levels - 1, tr : tr + 1])
        at = far + tr
        other_num = with_rows(other_last[tr], swept[at : at + 1], swept[at + tracers : at + tracers + 1])
        value = own_w * num + other_w * other_num
        adj_tracer[tr, level(levels - 1, depth, levels)] = value
        for j in range(levels - 2, -1, -1):
            num = with_rows(nums[j, tr], delta[0, j, tr : tr + 1], delta[1, j, tr : tr + 1])
            value = inverse[j] * num + ratio[j] * value
            adj_tracer[tr, level(j, depth, levels)] = value
    copy_out = pltpu.make_async_copy(adj_tracer, adj_tracer_out, sem)
    copy_out.start()

    parts = cols // 128
    lanes = [slice(128 * h, 128 * (h + 1)) for h in range(parts)]

    def place(ref, tile):
        for h, lane in enumerate(lanes):
            resid[h, pl.ds(tiles + tile, rows, stride=tiles)] = ref[0:rows, lane]
            damp[h, pl.ds(tile, rows, stride=tiles)] = 4.0 + ref[rows + 8 : 2 * rows + 8, lane]
            firsts[h, pl.ds(tile, 1)] = ref[rows : rows + 1, lane]
            finals[h, pl.ds(tile, 1)] = ref[rows + 1 : rows + 2, lane]

    place(own, me)
    for step, (for_top, for_bottom) in enumerate(partners):
        place(got[step], partner(me, jnp.where(depth == 0, for_top, for_bottom), tiles))
        place(swapped[step], partner(me, jnp.where(depth == 0, for_bottom, for_top), tiles))

    column = lax.broadcasted_iota(jnp.int32, (tiles, 128), 1)

    def group(ref, g):
        return [ref[h, g * tiles : (g + 1) * tiles] for h in range(parts)]

    def keep(ref, g, values):
        for h, value in enumerate(values):
            ref[h, g * tiles : (g + 1) * tiles] = value

    def beside(values):
        left = [pltpu.roll(v, 1, 1) for v in values]
        right = [pltpu.roll(v, 127, 1) for v in values]
        left = [jnp.where(column == 0, left[h - 1] if h > 0 else 0.0, left[h]) for h in range(parts)]
        right = [jnp.where(column == 127, right[h + 1] if h < parts - 1 else 0.0, right[h]) for h in range(parts)]
        return [p + q for p, q in zip(left, right)]

    for h in range(parts):
        next_first, _ = row_shifts(firsts[h], 0.0, 0.0)
        _, last_final = row_shifts(finals[h], 0.0, 0.0)
        resid[h, rows * tiles : (rows + 1) * tiles] += GRAVITY * next_first
        resid[h, tiles : 2 * tiles] -= GRAVITY * last_final

    def sweep(fresh):
        final, first = fresh(rows - 1), fresh(0)
        above = [row_shifts(v, 0.0, 0.0)[1] for v in final]
        after = [row_shifts(v, 0.0, 0.0)[0] for v in first]
        keep(resid, 0, above)
        keep(resid, rows + 1, after)
        norms = [jnp.zeros((tiles, 128), F32)] * parts
        dots = [jnp.zeros((tiles, 128), F32)] * parts
        here = first
        for b in range(rows):
            below = fresh(b + 1) if b + 1 < rows - 1 else final if b + 1 == rows - 1 else after
            side, weight = beside(here), group(damp, b)
            made = [weight[h] * here[h] - ((above[h] + below[h]) + side[h]) for h in range(parts)]
            keep(image, b, made)
            norms = [norms[h] + here[h] * here[h] for h in range(parts)]
            dots = [dots[h] + here[h] * made[h] for h in range(parts)]
            above, here = here, below
        return jnp.sum(sum(norms), keepdims=True), jnp.sum(sum(dots), keepdims=True)

    def step_own(alpha, beta):
        for h in range(parts):
            d = resid[h, pl.ds(me, rows + 2, stride=tiles)] + beta * direc[h]
            direc[h] = d
            sol[h] += alpha * d

    direc[...] = jnp.zeros_like(direc)
    sol[...] = jnp.zeros_like(sol)
    moved[...] = jnp.zeros_like(moved)
    norm, dot = sweep(lambda b: group(resid, b + 1))

    def advance(turn, carry):
        norm, alpha, beta = carry
        step_own(alpha, beta)

        def fresh(b):
            old, made, kept = group(resid, b + 1), group(image, b), group(moved, b)
            kept = [made[h] + beta * kept[h] for h in range(parts)]
            new = [old[h] - alpha * kept[h] for h in range(parts)]
            keep(moved, b, kept)
            keep(resid, b + 1, new)
            return new

        norm_now, dot = sweep(fresh)
        beta = norm_now / norm
        return norm_now, norm_now / (dot - beta * norm_now / alpha), beta

    _, alpha, beta = lax.fori_loop(0, ITERS - 1, advance, (norm, norm / dot, jnp.zeros_like(norm)))
    step_own(alpha, beta)

    x = jnp.concatenate([sol[h, 1 : rows + 1] for h in range(parts)], axis=1)
    adj_surface[...] = x
    right, left = lane_shifts(x)
    slope_x = ADVECT * (right - left)
    slope_y = jnp.concatenate([ADVECT * (sol[h, 2 : rows + 2] - sol[h, 0:rows]) for h in range(parts)], axis=1)
    for lev in range(levels):
        adj_velocity[0, lev] = flux[0, lev] + slope_x
        adj_velocity[1, lev] = flux[1, lev] + slope_y
    copy_out.wait()


def solve_call(partners, args, tiles):
    flux, last = args[0], args[3]
    tracers = last.shape[0]
    levels, rows, cols = flux.shape[1:]
    plane, height, parts = (rows, cols), tiles * rows, cols // 128
    block = (tracers, levels) + plane
    return call(
        functools.partial(solve_kernel, tiles, partners),
        [block, (2, levels) + plane, plane],
        args,
        scratch=[
            pltpu.VMEM((parts, height + 2 * tiles, 128), F32),
            pltpu.VMEM((parts, height, 128), F32),
            pltpu.VMEM((parts, height, 128), F32),
            pltpu.VMEM((parts, height, 128), F32),
            pltpu.VMEM((parts, tiles, 128), F32),
            pltpu.VMEM((parts, tiles, 128), F32),
            pltpu.VMEM((parts, rows + 2, 128), F32),
            pltpu.VMEM((parts, rows + 2, 128), F32),
            pltpu.VMEM(block, F32),
            pltpu.SemaphoreType.DMA(()),
        ],
        hbm_out=(0,),
    )


def partner(tile, offset, tiles):
    if tiles & (tiles - 1) == 0:
        return tile ^ offset
    return (offset + tiles - tile) % tiles


def partner_offsets(tiles):
    if tiles & (tiles - 1) == 0:
        others = list(range(1, tiles))
    else:
        others = list(range(tiles))
    if len(others) % 2 == 1:
        others = others[:1] + others
    pairs = [(others[i], others[i + 1]) for i in range(0, len(others), 2)]
    return [pair if i % 2 == 0 else pair[::-1] for i, pair in enumerate(pairs)]


def body(tracer_start, velocity, surface, mixing, land_mask, damping, tracer_cot, surface_cot):
    tracers, levels, rows, cols = tracer_start.shape
    tiles = lax.axis_size("tile")
    swap = [(0, 1), (1, 0)]
    plane = (rows, cols)
    block = (tracers, levels) + plane
    edge = (tracers * levels + 8, cols)
    face, edge_b, edge_a = call(
        start_kernel,
        [(tracers + 2,) + plane, edge, edge],
        [tracer_start, mixing, tracer_cot, land_mask, surface],
        scratch=[
            pltpu.VMEM(block, F32),
            pltpu.VMEM((levels,) + plane, F32),
            pltpu.VMEM(plane, F32),
            pltpu.VMEM((2, tracers, levels, 8, cols), F32),
            pltpu.VMEM((levels,) + plane, jnp.int32),
            pltpu.SemaphoreType.DMA((6,)),
        ],
        hbm_in=range(5),
        vmem=56,
    )
    pairs_a = [(i, i + 1) for i in range(0, tiles - 1, 2)]
    pairs_b = [(i, i + 1) for i in range(1, tiles - 1, 2)]
    other = lax.ppermute(face, "depth", swap)
    edge_b = lax.ppermute(edge_b, "tile", pairs_b + [(b, a) for a, b in pairs_b])
    edge_a = lax.ppermute(edge_a, "tile", pairs_a + [(b, a) for a, b in pairs_a])
    planes = tracers * levels
    flux, nums, last, packed, lines = call(
        interior_kernel,
        [(2, levels) + plane, (levels - 1, tracers) + plane, (tracers,) + plane, (4, planes, cols), (4 * levels, cols)],
        [tracer_start, mixing, tracer_cot, land_mask, velocity, surface, other],
        scratch=[pltpu.VMEM((2, levels) + plane, F32)],
    )
    other_last = lax.ppermute(last, "depth", swap)
    flux, delta, part = call(
        column_kernel,
        [(2, levels) + plane, (2, levels, tracers, cols), (2 * rows + 8 + 2 * tracers, cols)],
        [flux, packed, lines, edge_b, edge_a, surface_cot, damping],
    )
    swept = lax.ppermute(part, "depth", swap)
    own = part[: 2 * rows + 8] + swept[: 2 * rows + 8]

    partners = partner_offsets(tiles)
    got = []
    for for_top, for_bottom in partners:
        pairs = [(2 * partner(t, for_top, tiles), 2 * t) for t in range(tiles)]
        pairs += [(2 * partner(t, for_bottom, tiles) + 1, 2 * t + 1) for t in range(tiles)]
        got.append(lax.ppermute(own, ("tile", "depth"), pairs))
    swapped = [lax.ppermute(piece, "depth", swap) for piece in got]

    return solve_call(
        partners,
        [flux, mixing, nums, last, delta, other, other_last, swept, own] + got + swapped,
        tiles,
    )


def solution(mesh):
    return jax.shard_map(
        body,
        mesh=mesh,
        in_specs=(
            P("grp", "depth", "tile", None),
            P("grp", "depth", "tile", None),
            P(("grp", "tile"), None),
            P(("grp", "depth"), "tile", None),
            P("depth", "tile", None),
            P("tile", None),
            P("grp", "depth", "tile", None),
            P(("grp", "tile"), None),
        ),
        out_specs=(
            P("grp", "depth", "tile", None),
            P("grp", "depth", "tile", None),
            P(("grp", "tile"), None),
        ),
        check_vma=False,
    )
```

```python
import functools

import jax
import jax.numpy as jnp
from jax import lax
from jax.experimental import pallas as pl
from jax.experimental.pallas import tpu as pltpu
from jax.sharding import PartitionSpec as P

ITERS = 6
ADVECT = 0.25
DIFFUSE = 0.1
GRAVITY = 0.5

F32 = jnp.float32
VMEM = pl.BlockSpec(memory_space=pltpu.VMEM)
HBM = pl.BlockSpec(memory_space=pltpu.HBM)


def call(kernel, outs, args, scratch=(), flops=2_000_000, hbm_in=(), hbm_out=(), vmem=40):
    nbytes = sum(a.size * 4 for a in args) + sum(4 * functools.reduce(lambda p, q: p * q, s) for s in outs)
    return pl.pallas_call(
        kernel,
        out_shape=[jax.ShapeDtypeStruct(s, F32) for s in outs],
        in_specs=[HBM if i in hbm_in else VMEM for i in range(len(args))],
        out_specs=[HBM if i in hbm_out else VMEM for i in range(len(outs))],
        scratch_shapes=list(scratch),
        cost_estimate=pl.CostEstimate(flops=flops, bytes_accessed=nbytes, transcendentals=0),
        compiler_params=pltpu.CompilerParams(vmem_limit_bytes=int(vmem * 1024 * 1024)),
    )(*args)


def lane_shifts(f):
    lane = lax.broadcasted_iota(jnp.int32, f.shape, f.ndim - 1)
    cols = f.shape[-1]
    after = jnp.where(lane == cols - 1, 0.0, pltpu.roll(f, cols - 1, f.ndim - 1))
    before = jnp.where(lane == 0, 0.0, pltpu.roll(f, 1, f.ndim - 1))
    return after, before


def row_shifts(f, low, high):
    row = lax.broadcasted_iota(jnp.int32, f.shape, 0)
    rows = f.shape[0]
    after = jnp.where(row == rows - 1, high, pltpu.roll(f, rows - 1, 0))
    before = jnp.where(row == 0, low, pltpu.roll(f, 1, 0))
    return after, before


def chain(mix_ref, depth):
    levels = mix_ref.shape[0]
    links = [mix_ref[j + depth * (levels - 2 - 2 * j)] for j in range(levels - 1)]
    rest = jnp.ones_like(links[0])
    inverse, ratio = [], []
    for link in links:
        inv = 1.0 / (rest + link)
        inverse.append(inv)
        ratio.append(link * inv)
        rest = 1.0 + link * (rest * inv)
    return inverse, ratio, rest


def level(j, depth, levels):
    return j + depth * (levels - 1 - 2 * j)


def meet(rest, other_rest, own_mix, other_mix, depth):
    link = jnp.where(depth == 0, own_mix, other_mix)
    det = rest * other_rest + link * (rest + other_rest)
    inv = 1.0 / det
    return (other_rest + link) * inv, link * inv


def edge_kernel(cot_in, mask_in, surface_in, tracer_in, mix_in, velocity_in, edge_b, edge_a, cot, mask, surface, sems):
    levels, rows, _ = mask_in.shape
    tracers = cot_in.shape[0] // levels
    odd = lax.rem(lax.axis_index("tile"), 2) == 1
    copies = []
    for side, start in enumerate((0, rows - 8)):
        part = pl.ds(start, 8)
        moves = [(cot_in.at[:, part], cot), (mask_in.at[:, part], mask), (surface_in.at[part], surface)]
        for src, dst in moves:
            copies.append(pltpu.make_async_copy(src, dst.at[side], sems.at[len(copies)]))
    for copy in copies:
        copy.start()
    for copy in copies:
        copy.wait()
    for lev in range(levels):
        first_wet = mask[0, lev, 0:1].astype(F32)
        last_wet = mask[1, lev, 7:8].astype(F32)
        for tr in range(tracers):
            first = cot[0, tr * levels + lev, 0:1] * first_wet
            last = cot[1, tr * levels + lev, 7:8] * last_wet
            at = lev * tracers + tr
            edge_a[at : at + 1] = jnp.where(odd, first, last)
            edge_b[at : at + 1] = jnp.where(odd, last, first)
    at = tracers * levels
    edge_a[at : at + 8] = jnp.zeros_like(edge_a[at : at + 8])
    edge_b[at : at + 8] = jnp.zeros_like(edge_b[at : at + 8])
    first, last = surface[0, 0:1], surface[1, 7:8]
    edge_a[at : at + 1] = jnp.where(odd, first, last)
    edge_b[at : at + 1] = jnp.where(odd, last, first)


def interior_kernel(tracer, mix, cot, mask, velocity, surface, other, other_mix, flux, nums, last, packed, lines, speed):
    tracers, levels, rows, cols = tracer.shape
    depth = lax.axis_index("depth")
    inverse, ratio, rest = chain(mix, depth)
    _, other_ratio, other_rest = chain(other_mix, 1 - depth)
    own_w, other_w = meet(rest, other_rest, mix[levels - 1], other_mix[levels - 1], depth)
    right, left = lane_shifts(surface[...])
    down, up = row_shifts(surface[...], 0.0, 0.0)
    for lev in range(levels):
        speed[0, lev] = ADVECT * (velocity[0, lev] - GRAVITY * (right - left))
        along = ADVECT * (velocity[1, lev] - GRAVITY * (down - up))
        speed[1, lev] = along
        lines[lev : lev + 1] = along[0:1]
        lines[levels + lev : levels + lev + 1] = along[rows - 1 : rows]
    lines[2 * levels : 4 * levels] = jnp.zeros((2 * levels, cols), F32)
    for j in range(levels - 1):
        at = 2 * levels + j
        lines[at : at + 1] = ratio[j][0:1]
        lines[at + levels : at + levels + 1] = ratio[j][rows - 1 : rows]
    flux[...] = jnp.zeros_like(flux)
    for tr in range(tracers):
        held = [tracer[tr, level(0, depth, levels)]]
        for j in range(1, levels):
            held.append(tracer[tr, level(j, depth, levels)] + ratio[j - 1] * held[-1])
        met = other[tr, level(0, 1 - depth, levels)]
        for j in range(1, levels):
            met = other[tr, level(j, 1 - depth, levels)] + other_ratio[j - 1] * met
        value = own_w * held[-1] + other_w * met
        outs = [None] * levels
        for j in range(levels - 1, -1, -1):
            lev = level(j, depth, levels)
            if j < levels - 1:
                value = inverse[j] * held[j] + ratio[j] * value
            block = cot[tr, lev] * mask[lev].astype(F32)
            right, left = lane_shifts(block)
            down, up = row_shifts(block, 0.0, 0.0)
            across, along = right - left, down - up
            flux[0, lev] += ADVECT * (value * across)
            flux[1, lev] += ADVECT * (value * along)
            outs[j] = (
                block
                + (speed[0, lev] * across + speed[1, lev] * along)
                + DIFFUSE * (down + up + right + left - 4.0 * block)
            )
            at = lev * tracers + tr
            packed[0, pl.ds(at, 1)] = value[0:1]
            packed[1, pl.ds(at, 1)] = value[rows - 1 : rows]
            packed[2, pl.ds(at, 1)] = block[1:2]
            packed[3, pl.ds(at, 1)] = block[rows - 2 : rows - 1]
        num = outs[0]
        for j in range(1, levels):
            nums[j - 1, tr] = num
            num = outs[j] + ratio[j - 1] * num
        last[tr] = num


def column_kernel(flux_in, packed, lines, edge_b, edge_a, surface_cot, damping, flux, delta, send):
    levels, rows, cols = flux.shape[1:]
    tracers = delta.shape[2]
    depth = lax.axis_index("depth")
    odd = lax.rem(lax.axis_index("tile"), 2) == 1
    row = lax.broadcasted_iota(jnp.int32, (rows, cols), 0)
    kind = lax.broadcasted_iota(jnp.int32, (8, cols), 0)

    def halo(at, size):
        from_a, from_b = edge_a[pl.ds(at, size)], edge_b[pl.ds(at, size)]
        return jnp.where(odd, from_a, from_b), jnp.where(odd, from_b, from_a)

    col_x = jnp.zeros((rows, cols), F32)
    col_y = jnp.zeros((rows, cols), F32)
    for lev in range(levels):
        low, high = halo(lev * tracers, tracers)
        at = slice(lev * tracers, (lev + 1) * tracers)
        minus = ADVECT * jnp.sum(packed[0, at] * low, axis=0, keepdims=True)
        plus = ADVECT * jnp.sum(packed[1, at] * high, axis=0, keepdims=True)
        flux_x = flux_in[0, lev]
        flux_y = flux_in[1, lev] + (jnp.where(row == rows - 1, plus, 0.0) - jnp.where(row == 0, minus, 0.0))
        flux[0, lev] = flux_x
        flux[1, lev] = flux_y
        col_x += flux_x
        col_y += flux_y
    right, left = lane_shifts(col_x)
    down, up = row_shifts(col_y, 0.0, 0.0)
    top = depth == 0
    source = GRAVITY * (right - left + down - up)
    send[0:rows] = source + jnp.where(top, surface_cot[...], 0.0)
    send[rows : rows + 8] = jnp.where(kind == 0, col_y[0:1], jnp.where(kind == 1, col_y[rows - 1 : rows], 0.0))
    send[rows + 8 : 2 * rows + 8] = jnp.where(top, damping[...], 0.0)

    low_s, high_s = halo(levels * tracers, 8)
    low_s, high_s = ADVECT * GRAVITY * low_s[0:1], ADVECT * GRAVITY * high_s[0:1]
    for j in range(levels):
        lev = level(j, depth, levels)
        at = pl.multiple_of(lev * tracers, tracers)
        low, high = halo(at, tracers)
        first = low_s * packed[2, pl.ds(at, tracers)] + (DIFFUSE - (lines[pl.ds(lev, 1)] + low_s)) * low
        final = high_s * packed[3, pl.ds(at, tracers)] + (DIFFUSE + (lines[pl.ds(levels + lev, 1)] - high_s)) * high
        if j > 0:
            first = first + lines[2 * levels + j - 1 : 2 * levels + j] * delta[0, j - 1]
            final = final + lines[3 * levels + j - 1 : 3 * levels + j] * delta[1, j - 1]
        delta[0, j] = first
        delta[1, j] = final
    send[2 * rows + 8 : 2 * rows + 8 + tracers] = delta[0, levels - 1]
    send[2 * rows + 8 + tracers : 2 * rows + 8 + 2 * tracers] = delta[1, levels - 1]


def solve_kernel(tiles, partners, flux, mix, nums, last, delta, other_mix, other_last, swept, own, *refs):
    steps = len(partners)
    got, swapped = refs[:steps], refs[steps : 2 * steps]
    adj_tracer_out, adj_velocity, adj_surface = refs[2 * steps : 2 * steps + 3]
    resid, image, moved, damp, firsts, finals, direc, sol, adj_tracer, sem = refs[2 * steps + 3 :]
    levels, rows, cols = flux.shape[1:]
    me = lax.axis_index("tile")
    depth = lax.axis_index("depth")

    tracers = last.shape[0]
    inverse, ratio, rest = chain(mix, depth)
    _, _, other_rest = chain(other_mix, 1 - depth)
    own_w, other_w = meet(rest, other_rest, mix[levels - 1], other_mix[levels - 1], depth)
    row = lax.broadcasted_iota(jnp.int32, (rows, cols), 0)
    far = 2 * rows + 8

    def with_rows(block, first, final):
        return block + (jnp.where(row == 0, first, 0.0) + jnp.where(row == rows - 1, final, 0.0))

    for tr in range(tracers):
        num = with_rows(last[tr], delta[0, levels - 1, tr : tr + 1], delta[1, levels - 1, tr : tr + 1])
        at = far + tr
        other_num = with_rows(other_last[tr], swept[at : at + 1], swept[at + tracers : at + tracers + 1])
        value = own_w * num + other_w * other_num
        adj_tracer[tr, level(levels - 1, depth, levels)] = value
        for j in range(levels - 2, -1, -1):
            num = with_rows(nums[j, tr], delta[0, j, tr : tr + 1], delta[1, j, tr : tr + 1])
            value = inverse[j] * num + ratio[j] * value
            adj_tracer[tr, level(j, depth, levels)] = value
    copy_out = pltpu.make_async_copy(adj_tracer, adj_tracer_out, sem)
    copy_out.start()

    parts = cols // 128
    lanes = [slice(128 * h, 128 * (h + 1)) for h in range(parts)]

    def place(ref, tile):
        for h, lane in enumerate(lanes):
            resid[h, pl.ds(tiles + tile, rows, stride=tiles)] = ref[0:rows, lane]
            damp[h, pl.ds(tile, rows, stride=tiles)] = 4.0 + ref[rows + 8 : 2 * rows + 8, lane]
            firsts[h, pl.ds(tile, 1)] = ref[rows : rows + 1, lane]
            finals[h, pl.ds(tile, 1)] = ref[rows + 1 : rows + 2, lane]

    place(own, me)
    for step, (for_top, for_bottom) in enumerate(partners):
        place(got[step], partner(me, jnp.where(depth == 0, for_top, for_bottom), tiles))
        place(swapped[step], partner(me, jnp.where(depth == 0, for_bottom, for_top), tiles))

    column = lax.broadcasted_iota(jnp.int32, (tiles, 128), 1)

    def group(ref, g):
        return [ref[h, g * tiles : (g + 1) * tiles] for h in range(parts)]

    def keep(ref, g, values):
        for h, value in enumerate(values):
            ref[h, g * tiles : (g + 1) * tiles] = value

    def beside(values):
        left = [pltpu.roll(v, 1, 1) for v in values]
        right = [pltpu.roll(v, 127, 1) for v in values]
        left = [jnp.where(column == 0, left[h - 1] if h > 0 else 0.0, left[h]) for h in range(parts)]
        right = [jnp.where(column == 127, right[h + 1] if h < parts - 1 else 0.0, right[h]) for h in range(parts)]
        return [p + q for p, q in zip(left, right)]

    for h in range(parts):
        next_first, _ = row_shifts(firsts[h], 0.0, 0.0)
        _, last_final = row_shifts(finals[h], 0.0, 0.0)
        resid[h, rows * tiles : (rows + 1) * tiles] += GRAVITY * next_first
        resid[h, tiles : 2 * tiles] -= GRAVITY * last_final

    def sweep(fresh):
        final, first = fresh(rows - 1), fresh(0)
        above = [row_shifts(v, 0.0, 0.0)[1] for v in final]
        after = [row_shifts(v, 0.0, 0.0)[0] for v in first]
        keep(resid, 0, above)
        keep(resid, rows + 1, after)
        norms = [jnp.zeros((tiles, 128), F32)] * parts
        dots = [jnp.zeros((tiles, 128), F32)] * parts
        here = first
        for b in range(rows):
            below = fresh(b + 1) if b + 1 < rows - 1 else final if b + 1 == rows - 1 else after
            side, weight = beside(here), group(damp, b)
            made = [weight[h] * here[h] - ((above[h] + below[h]) + side[h]) for h in range(parts)]
            keep(image, b, made)
            norms = [norms[h] + here[h] * here[h] for h in range(parts)]
            dots = [dots[h] + here[h] * made[h] for h in range(parts)]
            above, here = here, below
        return jnp.sum(sum(norms), keepdims=True), jnp.sum(sum(dots), keepdims=True)

    def step_own(alpha, beta):
        for h in range(parts):
            d = resid[h, pl.ds(me, rows + 2, stride=tiles)] + beta * direc[h]
            direc[h] = d
            sol[h] += alpha * d

    direc[...] = jnp.zeros_like(direc)
    sol[...] = jnp.zeros_like(sol)
    moved[...] = jnp.zeros_like(moved)
    norm, dot = sweep(lambda b: group(resid, b + 1))

    def advance(turn, carry):
        over_norm, inv, alpha, beta = carry
        step_own(alpha, beta)

        def fresh(b):
            old, made, kept = group(resid, b + 1), group(image, b), group(moved, b)
            kept = [made[h] + beta * kept[h] for h in range(parts)]
            new = [old[h] - alpha * kept[h] for h in range(parts)]
            keep(moved, b, kept)
            keep(resid, b + 1, new)
            return new

        norm, dot = sweep(fresh)
        beta = norm * over_norm
        divisor = dot - norm * (beta * inv)
        over_norm = 1.0 / norm
        return over_norm, divisor * over_norm, norm / divisor, beta

    over_norm = 1.0 / norm
    first = (over_norm, dot * over_norm, norm / dot, jnp.zeros_like(norm))
    _, _, alpha, beta = lax.fori_loop(0, ITERS - 1, advance, first)
    step_own(alpha, beta)

    x = jnp.concatenate([sol[h, 1 : rows + 1] for h in range(parts)], axis=1)
    adj_surface[...] = x
    right, left = lane_shifts(x)
    slope_x = ADVECT * (right - left)
    slope_y = jnp.concatenate([ADVECT * (sol[h, 2 : rows + 2] - sol[h, 0:rows]) for h in range(parts)], axis=1)
    for lev in range(levels):
        adj_velocity[0, lev] = flux[0, lev] + slope_x
        adj_velocity[1, lev] = flux[1, lev] + slope_y
    copy_out.wait()


def solve_call(partners, args, tiles):
    flux, last = args[0], args[3]
    tracers = last.shape[0]
    levels, rows, cols = flux.shape[1:]
    plane, height, parts = (rows, cols), tiles * rows, cols // 128
    block = (tracers, levels) + plane
    return call(
        functools.partial(solve_kernel, tiles, partners),
        [block, (2, levels) + plane, plane],
        args,
        scratch=[
            pltpu.VMEM((parts, height + 2 * tiles, 128), F32),
            pltpu.VMEM((parts, height, 128), F32),
            pltpu.VMEM((parts, height, 128), F32),
            pltpu.VMEM((parts, height, 128), F32),
            pltpu.VMEM((parts, tiles, 128), F32),
            pltpu.VMEM((parts, tiles, 128), F32),
            pltpu.VMEM((parts, rows + 2, 128), F32),
            pltpu.VMEM((parts, rows + 2, 128), F32),
            pltpu.VMEM(block, F32),
            pltpu.SemaphoreType.DMA(()),
        ],
        hbm_out=(0,),
    )


def partner(tile, offset, tiles):
    if tiles & (tiles - 1) == 0:
        return tile ^ offset
    return (offset + tiles - tile) % tiles


def partner_offsets(tiles):
    if tiles & (tiles - 1) == 0:
        others = sorted(range(1, tiles), key=lambda k: (bin(k).count("1"), k))
    else:
        others = list(range(tiles))
    if len(others) % 2 == 1:
        others = others[:1] + others
    return [(others[i], others[i + 1]) for i in range(0, len(others), 2)]


def body(tracer_start, velocity, surface, mixing, land_mask, damping, tracer_cot, surface_cot):
    tracers, levels, rows, cols = tracer_start.shape
    tiles = lax.axis_size("tile")
    swap = [(0, 1), (1, 0)]
    plane = (rows, cols)
    block = (tracers, levels) + plane
    edge = (tracers * levels + 8, cols)
    edge_b, edge_a = call(
        edge_kernel,
        [edge, edge],
        [tracer_cot.reshape(tracers * levels, rows, cols), land_mask, surface, tracer_start, mixing, velocity],
        scratch=[
            pltpu.VMEM((2, tracers * levels, 8, cols), F32),
            pltpu.VMEM((2, levels, 8, cols), jnp.int32),
            pltpu.VMEM((2, 8, cols), F32),
            pltpu.SemaphoreType.DMA((6,)),
        ],
        hbm_in=range(6),
        vmem=56,
    )
    pairs_a = [(i, i + 1) for i in range(0, tiles - 1, 2)]
    pairs_b = [(i, i + 1) for i in range(1, tiles - 1, 2)]
    other = lax.ppermute(tracer_start, "depth", swap)
    other_mix = lax.ppermute(mixing, "depth", swap)
    edge_b = lax.ppermute(edge_b, "tile", pairs_b + [(b, a) for a, b in pairs_b])
    edge_a = lax.ppermute(edge_a, "tile", pairs_a + [(b, a) for a, b in pairs_a])
    planes = tracers * levels
    flux, nums, last, packed, lines = call(
        interior_kernel,
        [(2, levels) + plane, (levels - 1, tracers) + plane, (tracers,) + plane, (4, planes, cols), (4 * levels, cols)],
        [tracer_start, mixing, tracer_cot, land_mask, velocity, surface, other, other_mix],
        scratch=[pltpu.VMEM((2, levels) + plane, F32)],
    )
    flux, delta, part = call(
        column_kernel,
        [(2, levels) + plane, (2, levels, tracers, cols), (2 * rows + 8 + 2 * tracers, cols)],
        [flux, packed, lines, edge_b, edge_a, surface_cot, damping],
    )
    swept = lax.ppermute(part, "depth", swap)
    own = part[: 2 * rows + 8] + swept[: 2 * rows + 8]

    partners = partner_offsets(tiles)
    got = []
    for for_top, for_bottom in partners:
        pairs = [(2 * partner(t, for_top, tiles), 2 * t) for t in range(tiles)]
        pairs += [(2 * partner(t, for_bottom, tiles) + 1, 2 * t + 1) for t in range(tiles)]
        got.append(lax.ppermute(own, ("tile", "depth"), pairs))
    swapped = [lax.ppermute(piece, "depth", swap) for piece in got]

    last_late, _ = lax.optimization_barrier((last, own))
    other_last = lax.ppermute(last_late, "depth", swap)
    return solve_call(
        partners,
        [flux, mixing, nums, last, delta, other_mix, other_last, swept, own] + got + swapped,
        tiles,
    )


def solution(mesh):
    return jax.shard_map(
        body,
        mesh=mesh,
        in_specs=(
            P("grp", "depth", "tile", None),
            P("grp", "depth", "tile", None),
            P(("grp", "tile"), None),
            P(("grp", "depth"), "tile", None),
            P("depth", "tile", None),
            P("tile", None),
            P("grp", "depth", "tile", None),
            P(("grp", "tile"), None),
        ),
        out_specs=(
            P("grp", "depth", "tile", None),
            P("grp", "depth", "tile", None),
            P(("grp", "tile"), None),
        ),
        check_vma=False,
    )
```

```python
import functools

import jax
import jax.numpy as jnp
from jax import lax
from jax.experimental import pallas as pl
from jax.experimental.pallas import tpu as pltpu
from jax.sharding import PartitionSpec as P

ITERS = 6
ADVECT = 0.25
DIFFUSE = 0.1
GRAVITY = 0.5

F32 = jnp.float32
VMEM = pl.BlockSpec(memory_space=pltpu.VMEM)
HBM = pl.BlockSpec(memory_space=pltpu.HBM)


def call(kernel, outs, args, scratch=(), flops=2_000_000, hbm_in=(), hbm_out=(), near=False):
    nbytes = sum(a.size * 4 for a in args) + sum(4 * functools.reduce(lambda p, q: p * q, s) for s in outs)
    if near:
        args = [pltpu.with_memory_space_constraint(a, pltpu.HBM) for a in args]
    return pl.pallas_call(
        kernel,
        out_shape=[pltpu.VMEM(s, F32) if near else jax.ShapeDtypeStruct(s, F32) for s in outs],
        in_specs=[HBM if i in hbm_in else VMEM for i in range(len(args))],
        out_specs=[HBM if i in hbm_out else VMEM for i in range(len(outs))],
        scratch_shapes=list(scratch),
        cost_estimate=pl.CostEstimate(flops=flops, bytes_accessed=nbytes, transcendentals=0),
        compiler_params=pltpu.CompilerParams(vmem_limit_bytes=40 * 1024 * 1024),
    )(*args)


def lane_shifts(f):
    lane = lax.broadcasted_iota(jnp.int32, f.shape, f.ndim - 1)
    cols = f.shape[-1]
    after = jnp.where(lane == cols - 1, 0.0, pltpu.roll(f, cols - 1, f.ndim - 1))
    before = jnp.where(lane == 0, 0.0, pltpu.roll(f, 1, f.ndim - 1))
    return after, before


def row_shifts(f, low, high):
    row = lax.broadcasted_iota(jnp.int32, f.shape, 0)
    rows = f.shape[0]
    after = jnp.where(row == rows - 1, high, pltpu.roll(f, rows - 1, 0))
    before = jnp.where(row == 0, low, pltpu.roll(f, 1, 0))
    return after, before


def chain(mix_ref, depth):
    levels = mix_ref.shape[0]
    links = [mix_ref[j + depth * (levels - 2 - 2 * j)] for j in range(levels - 1)]
    rest = jnp.ones_like(links[0])
    inverse, ratio = [], []
    for link in links:
        inv = 1.0 / (rest + link)
        inverse.append(inv)
        ratio.append(link * inv)
        rest = 1.0 + link * (rest * inv)
    return inverse, ratio, rest


def level(j, depth, levels):
    return j + depth * (levels - 1 - 2 * j)


def meet(rest, other_rest, own_mix, other_mix, depth):
    link = jnp.where(depth == 0, own_mix, other_mix)
    det = rest * other_rest + link * (rest + other_rest)
    inv = 1.0 / det
    return (other_rest + link) * inv, link * inv


def edge_kernel(cot_in, mask_in, surface_in, tracer_in, mix_in, velocity_in, edge_b, edge_a, cot, mask, surface, sems):
    levels, rows, _ = mask_in.shape
    tracers = cot_in.shape[0] // levels
    odd = lax.rem(lax.axis_index("tile"), 2) == 1
    copies = []
    for side, start in enumerate((0, rows - 8)):
        part = pl.ds(start, 8)
        moves = [(cot_in.at[:, part], cot), (mask_in.at[:, part], mask), (surface_in.at[part], surface)]
        for src, dst in moves:
            copies.append(pltpu.make_async_copy(src, dst.at[side], sems.at[len(copies)]))
    for copy in copies:
        copy.start()
    for copy in copies:
        copy.wait()
    for lev in range(levels):
        first_wet = mask[0, lev, 0:1].astype(F32)
        last_wet = mask[1, lev, 7:8].astype(F32)
        for tr in range(tracers):
            first = cot[0, tr * levels + lev, 0:1] * first_wet
            last = cot[1, tr * levels + lev, 7:8] * last_wet
            at = lev * tracers + tr
            edge_a[at : at + 1] = jnp.where(odd, first, last)
            edge_b[at : at + 1] = jnp.where(odd, last, first)
    at = tracers * levels
    edge_a[at : at + 8] = jnp.zeros_like(edge_a[at : at + 8])
    edge_b[at : at + 8] = jnp.zeros_like(edge_b[at : at + 8])
    first, last = surface[0, 0:1], surface[1, 7:8]
    edge_a[at : at + 1] = jnp.where(odd, first, last)
    edge_b[at : at + 1] = jnp.where(odd, last, first)


def interior_kernel(tracer, mix, cot, mask, velocity, surface, other, other_mix, flux, nums, last, packed, lines, speed):
    tracers, levels, rows, cols = tracer.shape
    depth = lax.axis_index("depth")
    inverse, ratio, rest = chain(mix, depth)
    _, other_ratio, other_rest = chain(other_mix, 1 - depth)
    own_w, other_w = meet(rest, other_rest, mix[levels - 1], other_mix[levels - 1], depth)
    right, left = lane_shifts(surface[...])
    down, up = row_shifts(surface[...], 0.0, 0.0)
    for lev in range(levels):
        speed[0, lev] = ADVECT * (velocity[0, lev] - GRAVITY * (right - left))
        along = ADVECT * (velocity[1, lev] - GRAVITY * (down - up))
        speed[1, lev] = along
        lines[lev : lev + 1] = along[0:1]
        lines[levels + lev : levels + lev + 1] = along[rows - 1 : rows]
    lines[2 * levels : 4 * levels] = jnp.zeros((2 * levels, cols), F32)
    for j in range(levels - 1):
        at = 2 * levels + j
        lines[at : at + 1] = ratio[j][0:1]
        lines[at + levels : at + levels + 1] = ratio[j][rows - 1 : rows]
    flux[...] = jnp.zeros_like(flux)
    for tr in range(tracers):
        held = [tracer[tr, level(0, depth, levels)]]
        for j in range(1, levels):
            held.append(tracer[tr, level(j, depth, levels)] + ratio[j - 1] * held[-1])
        met = other[tr, level(0, 1 - depth, levels)]
        for j in range(1, levels):
            met = other[tr, level(j, 1 - depth, levels)] + other_ratio[j - 1] * met
        value = own_w * held[-1] + other_w * met
        outs = [None] * levels
        for j in range(levels - 1, -1, -1):
            lev = level(j, depth, levels)
            if j < levels - 1:
                value = inverse[j] * held[j] + ratio[j] * value
            block = cot[tr, lev] * mask[lev].astype(F32)
            right, left = lane_shifts(block)
            down, up = row_shifts(block, 0.0, 0.0)
            across, along = right - left, down - up
            flux[0, lev] += ADVECT * (value * across)
            flux[1, lev] += ADVECT * (value * along)
            outs[j] = (
                block
                + (speed[0, lev] * across + speed[1, lev] * along)
                + DIFFUSE * (down + up + right + left - 4.0 * block)
            )
            at = lev * tracers + tr
            packed[0, pl.ds(at, 1)] = value[0:1]
            packed[1, pl.ds(at, 1)] = value[rows - 1 : rows]
            packed[2, pl.ds(at, 1)] = block[1:2]
            packed[3, pl.ds(at, 1)] = block[rows - 2 : rows - 1]
        num = outs[0]
        for j in range(1, levels):
            nums[j - 1, tr] = num
            num = outs[j] + ratio[j - 1] * num
        last[tr] = num


def column_kernel(flux_in, packed, lines, edge_b, edge_a, surface_cot, damping, flux, delta, send):
    levels, rows, cols = flux.shape[1:]
    tracers = delta.shape[2]
    depth = lax.axis_index("depth")
    odd = lax.rem(lax.axis_index("tile"), 2) == 1
    row = lax.broadcasted_iota(jnp.int32, (rows, cols), 0)
    kind = lax.broadcasted_iota(jnp.int32, (8, cols), 0)

    def halo(at, size):
        from_a, from_b = edge_a[pl.ds(at, size)], edge_b[pl.ds(at, size)]
        return jnp.where(odd, from_a, from_b), jnp.where(odd, from_b, from_a)

    col_x = jnp.zeros((rows, cols), F32)
    col_y = jnp.zeros((rows, cols), F32)
    for lev in range(levels):
        low, high = halo(lev * tracers, tracers)
        at = slice(lev * tracers, (lev + 1) * tracers)
        minus = ADVECT * jnp.sum(packed[0, at] * low, axis=0, keepdims=True)
        plus = ADVECT * jnp.sum(packed[1, at] * high, axis=0, keepdims=True)
        flux_x = flux_in[0, lev]
        flux_y = flux_in[1, lev] + (jnp.where(row == rows - 1, plus, 0.0) - jnp.where(row == 0, minus, 0.0))
        flux[0, lev] = flux_x
        flux[1, lev] = flux_y
        col_x += flux_x
        col_y += flux_y
    right, left = lane_shifts(col_x)
    down, up = row_shifts(col_y, 0.0, 0.0)
    top = depth == 0
    source = GRAVITY * (right - left + down - up)
    send[0:rows] = source + jnp.where(top, surface_cot[...], 0.0)
    send[rows : rows + 8] = jnp.where(kind == 0, col_y[0:1], jnp.where(kind == 1, col_y[rows - 1 : rows], 0.0))
    send[rows + 8 : 2 * rows + 8] = jnp.where(top, damping[...], 0.0)

    low_s, high_s = halo(levels * tracers, 8)
    low_s, high_s = ADVECT * GRAVITY * low_s[0:1], ADVECT * GRAVITY * high_s[0:1]
    for j in range(levels):
        lev = level(j, depth, levels)
        at = pl.multiple_of(lev * tracers, tracers)
        low, high = halo(at, tracers)
        first = low_s * packed[2, pl.ds(at, tracers)] + (DIFFUSE - (lines[pl.ds(lev, 1)] + low_s)) * low
        final = high_s * packed[3, pl.ds(at, tracers)] + (DIFFUSE + (lines[pl.ds(levels + lev, 1)] - high_s)) * high
        if j > 0:
            first = first + lines[2 * levels + j - 1 : 2 * levels + j] * delta[0, j - 1]
            final = final + lines[3 * levels + j - 1 : 3 * levels + j] * delta[1, j - 1]
        delta[0, j] = first
        delta[1, j] = final
    send[2 * rows + 8 : 2 * rows + 8 + tracers] = delta[0, levels - 1]
    send[2 * rows + 8 + tracers : 2 * rows + 8 + 2 * tracers] = delta[1, levels - 1]


def solve_kernel(tiles, partners, flux, mix, nums, last, delta, other_mix, other_last, swept, own, *refs):
    steps = len(partners)
    got, swapped = refs[:steps], refs[steps : 2 * steps]
    adj_tracer_out, adj_velocity, adj_surface = refs[2 * steps : 2 * steps + 3]
    resid, image, moved, damp, firsts, finals, direc, sol, adj_tracer, sem = refs[2 * steps + 3 :]
    levels, rows, cols = flux.shape[1:]
    me = lax.axis_index("tile")
    depth = lax.axis_index("depth")

    tracers = last.shape[0]
    inverse, ratio, rest = chain(mix, depth)
    _, _, other_rest = chain(other_mix, 1 - depth)
    own_w, other_w = meet(rest, other_rest, mix[levels - 1], other_mix[levels - 1], depth)
    row = lax.broadcasted_iota(jnp.int32, (rows, cols), 0)
    far = 2 * rows + 8

    def with_rows(block, first, final):
        return block + (jnp.where(row == 0, first, 0.0) + jnp.where(row == rows - 1, final, 0.0))

    for tr in range(tracers):
        num = with_rows(last[tr], delta[0, levels - 1, tr : tr + 1], delta[1, levels - 1, tr : tr + 1])
        at = far + tr
        other_num = with_rows(other_last[tr], swept[at : at + 1], swept[at + tracers : at + tracers + 1])
        value = own_w * num + other_w * other_num
        adj_tracer[tr, level(levels - 1, depth, levels)] = value
        for j in range(levels - 2, -1, -1):
            num = with_rows(nums[j, tr], delta[0, j, tr : tr + 1], delta[1, j, tr : tr + 1])
            value = inverse[j] * num + ratio[j] * value
            adj_tracer[tr, level(j, depth, levels)] = value
    copy_out = pltpu.make_async_copy(adj_tracer, adj_tracer_out, sem)
    copy_out.start()

    parts = cols // 128
    lanes = [slice(128 * h, 128 * (h + 1)) for h in range(parts)]

    def place(ref, tile):
        for h, lane in enumerate(lanes):
            resid[h, pl.ds(tiles + tile, rows, stride=tiles)] = ref[0:rows, lane]
            damp[h, pl.ds(tile, rows, stride=tiles)] = 4.0 + ref[rows + 8 : 2 * rows + 8, lane]
            firsts[h, pl.ds(tile, 1)] = ref[rows : rows + 1, lane]
            finals[h, pl.ds(tile, 1)] = ref[rows + 1 : rows + 2, lane]

    place(own, me)
    for step, (for_top, for_bottom) in enumerate(partners):
        place(got[step], partner(me, jnp.where(depth == 0, for_top, for_bottom), tiles))
        place(swapped[step], partner(me, jnp.where(depth == 0, for_bottom, for_top), tiles))

    column = lax.broadcasted_iota(jnp.int32, (tiles, 128), 1)

    def group(ref, g):
        return [ref[h, g * tiles : (g + 1) * tiles] for h in range(parts)]

    def keep(ref, g, values):
        for h, value in enumerate(values):
            ref[h, g * tiles : (g + 1) * tiles] = value

    def beside(values):
        left = [pltpu.roll(v, 1, 1) for v in values]
        right = [pltpu.roll(v, 127, 1) for v in values]
        left = [jnp.where(column == 0, left[h - 1] if h > 0 else 0.0, left[h]) for h in range(parts)]
        right = [jnp.where(column == 127, right[h + 1] if h < parts - 1 else 0.0, right[h]) for h in range(parts)]
        return [p + q for p, q in zip(left, right)]

    for h in range(parts):
        next_first, _ = row_shifts(firsts[h], 0.0, 0.0)
        _, last_final = row_shifts(finals[h], 0.0, 0.0)
        resid[h, rows * tiles : (rows + 1) * tiles] += GRAVITY * next_first
        resid[h, tiles : 2 * tiles] -= GRAVITY * last_final

    def sweep(fresh):
        final, first = fresh(rows - 1), fresh(0)
        above = [row_shifts(v, 0.0, 0.0)[1] for v in final]
        after = [row_shifts(v, 0.0, 0.0)[0] for v in first]
        keep(resid, 0, above)
        keep(resid, rows + 1, after)
        norms = [jnp.zeros((tiles, 128), F32)] * parts
        dots = [jnp.zeros((tiles, 128), F32)] * parts
        here = first
        for b in range(rows):
            below = fresh(b + 1) if b + 1 < rows - 1 else final if b + 1 == rows - 1 else after
            side, weight = beside(here), group(damp, b)
            made = [weight[h] * here[h] - ((above[h] + below[h]) + side[h]) for h in range(parts)]
            keep(image, b, made)
            norms = [norms[h] + here[h] * here[h] for h in range(parts)]
            dots = [dots[h] + here[h] * made[h] for h in range(parts)]
            above, here = here, below
        return jnp.sum(sum(norms), keepdims=True), jnp.sum(sum(dots), keepdims=True)

    def step_own(alpha, beta):
        for h in range(parts):
            d = resid[h, pl.ds(me, rows + 2, stride=tiles)] + beta * direc[h]
            direc[h] = d
            sol[h] += alpha * d

    direc[...] = jnp.zeros_like(direc)
    sol[...] = jnp.zeros_like(sol)
    moved[...] = jnp.zeros_like(moved)
    norm, dot = sweep(lambda b: group(resid, b + 1))

    def advance(turn, carry):
        over_norm, inv, alpha, beta = carry
        step_own(alpha, beta)

        def fresh(b):
            old, made, kept = group(resid, b + 1), group(image, b), group(moved, b)
            kept = [made[h] + beta * kept[h] for h in range(parts)]
            new = [old[h] - alpha * kept[h] for h in range(parts)]
            keep(moved, b, kept)
            keep(resid, b + 1, new)
            return new

        norm, dot = sweep(fresh)
        beta = norm * over_norm
        divisor = dot - norm * (beta * inv)
        over_norm = 1.0 / norm
        return over_norm, divisor * over_norm, norm / divisor, beta

    over_norm = 1.0 / norm
    first = (over_norm, dot * over_norm, norm / dot, jnp.zeros_like(norm))
    _, _, alpha, beta = lax.fori_loop(0, ITERS - 1, advance, first)
    step_own(alpha, beta)

    x = jnp.concatenate([sol[h, 1 : rows + 1] for h in range(parts)], axis=1)
    adj_surface[...] = x
    right, left = lane_shifts(x)
    slope_x = ADVECT * (right - left)
    slope_y = jnp.concatenate([ADVECT * (sol[h, 2 : rows + 2] - sol[h, 0:rows]) for h in range(parts)], axis=1)
    for lev in range(levels):
        adj_velocity[0, lev] = flux[0, lev] + slope_x
        adj_velocity[1, lev] = flux[1, lev] + slope_y
    copy_out.wait()


def solve_call(partners, args, tiles):
    flux, last = args[0], args[3]
    tracers = last.shape[0]
    levels, rows, cols = flux.shape[1:]
    plane, height, parts = (rows, cols), tiles * rows, cols // 128
    block = (tracers, levels) + plane
    return call(
        functools.partial(solve_kernel, tiles, partners),
        [block, (2, levels) + plane, plane],
        args,
        scratch=[
            pltpu.VMEM((parts, height + 2 * tiles, 128), F32),
            pltpu.VMEM((parts, height, 128), F32),
            pltpu.VMEM((parts, height, 128), F32),
            pltpu.VMEM((parts, height, 128), F32),
            pltpu.VMEM((parts, tiles, 128), F32),
            pltpu.VMEM((parts, tiles, 128), F32),
            pltpu.VMEM((parts, rows + 2, 128), F32),
            pltpu.VMEM((parts, rows + 2, 128), F32),
            pltpu.VMEM(block, F32),
            pltpu.SemaphoreType.DMA(()),
        ],
        hbm_out=(0,),
    )


def partner(tile, offset, tiles):
    if tiles & (tiles - 1) == 0:
        return tile ^ offset
    return (offset + tiles - tile) % tiles


def partner_offsets(tiles):
    if tiles & (tiles - 1) == 0:
        others = sorted(range(1, tiles), key=lambda k: (bin(k).count("1"), k))
    else:
        others = list(range(tiles))
    if len(others) % 2 == 1:
        others = others[:1] + others
    return [(others[i], others[i + 1]) for i in range(0, len(others), 2)]


def body(tracer_start, velocity, surface, mixing, land_mask, damping, tracer_cot, surface_cot):
    tracers, levels, rows, cols = tracer_start.shape
    tiles = lax.axis_size("tile")
    swap = [(0, 1), (1, 0)]
    plane = (rows, cols)
    block = (tracers, levels) + plane
    edge = (tracers * levels + 8, cols)
    edge_b, edge_a = call(
        edge_kernel,
        [edge, edge],
        [tracer_cot.reshape(tracers * levels, rows, cols), land_mask, surface, tracer_start, mixing, velocity],
        scratch=[
            pltpu.VMEM((2, tracers * levels, 8, cols), F32),
            pltpu.VMEM((2, levels, 8, cols), jnp.int32),
            pltpu.VMEM((2, 8, cols), F32),
            pltpu.SemaphoreType.DMA((6,)),
        ],
        hbm_in=range(6),
        near=True,
    )
    pairs_a = [(i, i + 1) for i in range(0, tiles - 1, 2)]
    pairs_b = [(i, i + 1) for i in range(1, tiles - 1, 2)]
    other = lax.ppermute(tracer_start, "depth", swap)
    other_mix = lax.ppermute(mixing, "depth", swap)
    edge_b = lax.ppermute(edge_b, "tile", pairs_b + [(b, a) for a, b in pairs_b])
    edge_a = lax.ppermute(edge_a, "tile", pairs_a + [(b, a) for a, b in pairs_a])
    planes = tracers * levels
    flux, nums, last, packed, lines = call(
        interior_kernel,
        [(2, levels) + plane, (levels - 1, tracers) + plane, (tracers,) + plane, (4, planes, cols), (4 * levels, cols)],
        [tracer_start, mixing, tracer_cot, land_mask, velocity, surface, other, other_mix],
        scratch=[pltpu.VMEM((2, levels) + plane, F32)],
    )
    flux, delta, part = call(
        column_kernel,
        [(2, levels) + plane, (2, levels, tracers, cols), (2 * rows + 8 + 2 * tracers, cols)],
        [flux, packed, lines, edge_b, edge_a, surface_cot, damping],
    )
    swept = lax.ppermute(part, "depth", swap)
    own = part[: 2 * rows + 8] + swept[: 2 * rows + 8]

    partners = partner_offsets(tiles)
    got = []
    for for_top, for_bottom in partners:
        pairs = [(2 * partner(t, for_top, tiles), 2 * t) for t in range(tiles)]
        pairs += [(2 * partner(t, for_bottom, tiles) + 1, 2 * t + 1) for t in range(tiles)]
        got.append(lax.ppermute(own, ("tile", "depth"), pairs))
    swapped = [lax.ppermute(piece, "depth", swap) for piece in got]

    last_late, _ = lax.optimization_barrier((last, own))
    other_last = lax.ppermute(last_late, "depth", swap)
    return solve_call(
        partners,
        [flux, mixing, nums, last, delta, other_mix, other_last, swept, own] + got + swapped,
        tiles,
    )


def solution(mesh):
    return jax.shard_map(
        body,
        mesh=mesh,
        in_specs=(
            P("grp", "depth", "tile", None),
            P("grp", "depth", "tile", None),
            P(("grp", "tile"), None),
            P(("grp", "depth"), "tile", None),
            P("depth", "tile", None),
            P("tile", None),
            P("grp", "depth", "tile", None),
            P(("grp", "tile"), None),
        ),
        out_specs=(
            P("grp", "depth", "tile", None),
            P("grp", "depth", "tile", None),
            P(("grp", "tile"), None),
        ),
        check_vma=False,
    )
```

```python
import functools

import jax
import jax.numpy as jnp
from jax import lax
from jax.experimental import pallas as pl
from jax.experimental.pallas import tpu as pltpu
from jax.sharding import PartitionSpec as P

ITERS = 6
ADVECT = 0.25
DIFFUSE = 0.1
GRAVITY = 0.5

F32 = jnp.float32
VMEM = pl.BlockSpec(memory_space=pltpu.VMEM)
HBM = pl.BlockSpec(memory_space=pltpu.HBM)


def call(kernel, outs, args, scratch=(), flops=2_000_000, hbm_in=(), hbm_out=(), near=False):
    nbytes = sum(a.size * 4 for a in args) + sum(4 * functools.reduce(lambda p, q: p * q, s) for s in outs)
    if near:
        args = [pltpu.with_memory_space_constraint(a, pltpu.HBM) for a in args]
    return pl.pallas_call(
        kernel,
        out_shape=[pltpu.VMEM(s, F32) if near else jax.ShapeDtypeStruct(s, F32) for s in outs],
        in_specs=[HBM if i in hbm_in else VMEM for i in range(len(args))],
        out_specs=[HBM if i in hbm_out else VMEM for i in range(len(outs))],
        scratch_shapes=list(scratch),
        cost_estimate=pl.CostEstimate(flops=flops, bytes_accessed=nbytes, transcendentals=0),
        compiler_params=pltpu.CompilerParams(vmem_limit_bytes=40 * 1024 * 1024),
    )(*args)


def lane_shifts(f):
    lane = lax.broadcasted_iota(jnp.int32, f.shape, f.ndim - 1)
    cols = f.shape[-1]
    after = jnp.where(lane == cols - 1, 0.0, pltpu.roll(f, cols - 1, f.ndim - 1))
    before = jnp.where(lane == 0, 0.0, pltpu.roll(f, 1, f.ndim - 1))
    return after, before


def row_shifts(f, low, high):
    row = lax.broadcasted_iota(jnp.int32, f.shape, 0)
    rows = f.shape[0]
    after = jnp.where(row == rows - 1, high, pltpu.roll(f, rows - 1, 0))
    before = jnp.where(row == 0, low, pltpu.roll(f, 1, 0))
    return after, before


def chain(mix_ref, depth):
    levels = mix_ref.shape[0]
    links = [mix_ref[j + depth * (levels - 2 - 2 * j)] for j in range(levels - 1)]
    rest = jnp.ones_like(links[0])
    inverse, ratio = [], []
    for link in links:
        inv = 1.0 / (rest + link)
        inverse.append(inv)
        ratio.append(link * inv)
        rest = 1.0 + link * (rest * inv)
    return inverse, ratio, rest


def level(j, depth, levels):
    return j + depth * (levels - 1 - 2 * j)


def meet(rest, other_rest, own_mix, other_mix, depth):
    link = jnp.where(depth == 0, own_mix, other_mix)
    det = rest * other_rest + link * (rest + other_rest)
    inv = 1.0 / det
    return (other_rest + link) * inv, link * inv


def edge_kernel(cot_in, mask_in, surface_in, tracer_in, mix_in, velocity_in, edge_b, edge_a, cot, mask, surface, sems):
    levels, rows, _ = mask_in.shape
    tracers = cot_in.shape[0] // levels
    odd = lax.rem(lax.axis_index("tile"), 2) == 1
    copies = []
    for side, start in enumerate((0, rows - 8)):
        part = pl.ds(start, 8)
        moves = [(cot_in.at[:, part], cot), (mask_in.at[:, part], mask), (surface_in.at[part], surface)]
        for src, dst in moves:
            copies.append(pltpu.make_async_copy(src, dst.at[side], sems.at[len(copies)]))
    for copy in copies:
        copy.start()
    for copy in copies:
        copy.wait()
    for lev in range(levels):
        first_wet = mask[0, lev, 0:1].astype(F32)
        last_wet = mask[1, lev, 7:8].astype(F32)
        for tr in range(tracers):
            first = cot[0, tr * levels + lev, 0:1] * first_wet
            last = cot[1, tr * levels + lev, 7:8] * last_wet
            at = lev * tracers + tr
            edge_a[at : at + 1] = jnp.where(odd, first, last)
            edge_b[at : at + 1] = jnp.where(odd, last, first)
    at = tracers * levels
    edge_a[at : at + 8] = jnp.zeros_like(edge_a[at : at + 8])
    edge_b[at : at + 8] = jnp.zeros_like(edge_b[at : at + 8])
    first, last = surface[0, 0:1], surface[1, 7:8]
    edge_a[at : at + 1] = jnp.where(odd, first, last)
    edge_b[at : at + 1] = jnp.where(odd, last, first)


def interior_kernel(tracer, mix, cot, mask, velocity, surface, other, other_mix, flux, nums, last, packed, lines, speed):
    tracers, levels, rows, cols = tracer.shape
    depth = lax.axis_index("depth")
    inverse, ratio, rest = chain(mix, depth)
    _, other_ratio, other_rest = chain(other_mix, 1 - depth)
    own_w, other_w = meet(rest, other_rest, mix[levels - 1], other_mix[levels - 1], depth)
    right, left = lane_shifts(surface[...])
    down, up = row_shifts(surface[...], 0.0, 0.0)
    for lev in range(levels):
        speed[0, lev] = ADVECT * (velocity[0, lev] - GRAVITY * (right - left))
        along = ADVECT * (velocity[1, lev] - GRAVITY * (down - up))
        speed[1, lev] = along
        lines[lev : lev + 1] = along[0:1]
        lines[levels + lev : levels + lev + 1] = along[rows - 1 : rows]
    lines[2 * levels : 4 * levels] = jnp.zeros((2 * levels, cols), F32)
    for j in range(levels - 1):
        at = 2 * levels + j
        lines[at : at + 1] = ratio[j][0:1]
        lines[at + levels : at + levels + 1] = ratio[j][rows - 1 : rows]
    flux[...] = jnp.zeros_like(flux)
    for tr in range(tracers):
        held = [tracer[tr, level(0, depth, levels)]]
        for j in range(1, levels):
            held.append(tracer[tr, level(j, depth, levels)] + ratio[j - 1] * held[-1])
        met = other[tr, level(0, 1 - depth, levels)]
        for j in range(1, levels):
            met = other[tr, level(j, 1 - depth, levels)] + other_ratio[j - 1] * met
        value = own_w * held[-1] + other_w * met
        outs = [None] * levels
        for j in range(levels - 1, -1, -1):
            lev = level(j, depth, levels)
            if j < levels - 1:
                value = inverse[j] * held[j] + ratio[j] * value
            block = cot[tr, lev] * mask[lev].astype(F32)
            right, left = lane_shifts(block)
            down, up = row_shifts(block, 0.0, 0.0)
            across, along = right - left, down - up
            flux[0, lev] += ADVECT * (value * across)
            flux[1, lev] += ADVECT * (value * along)
            outs[j] = (
                block
                + (speed[0, lev] * across + speed[1, lev] * along)
                + DIFFUSE * (down + up + right + left - 4.0 * block)
            )
            at = lev * tracers + tr
            packed[0, pl.ds(at, 1)] = value[0:1]
            packed[1, pl.ds(at, 1)] = value[rows - 1 : rows]
            packed[2, pl.ds(at, 1)] = block[1:2]
            packed[3, pl.ds(at, 1)] = block[rows - 2 : rows - 1]
        num = outs[0]
        for j in range(1, levels):
            nums[j - 1, tr] = num
            num = outs[j] + ratio[j - 1] * num
        last[tr] = num


def column_kernel(flux_in, packed, lines, edge_b, edge_a, surface_cot, damping, flux, delta, send):
    levels, rows, cols = flux.shape[1:]
    tracers = delta.shape[2]
    depth = lax.axis_index("depth")
    odd = lax.rem(lax.axis_index("tile"), 2) == 1
    row = lax.broadcasted_iota(jnp.int32, (rows, cols), 0)
    kind = lax.broadcasted_iota(jnp.int32, (8, cols), 0)

    def halo(at, size):
        from_a, from_b = edge_a[pl.ds(at, size)], edge_b[pl.ds(at, size)]
        return jnp.where(odd, from_a, from_b), jnp.where(odd, from_b, from_a)

    col_x = jnp.zeros((rows, cols), F32)
    col_y = jnp.zeros((rows, cols), F32)
    for lev in range(levels):
        low, high = halo(lev * tracers, tracers)
        at = slice(lev * tracers, (lev + 1) * tracers)
        minus = ADVECT * jnp.sum(packed[0, at] * low, axis=0, keepdims=True)
        plus = ADVECT * jnp.sum(packed[1, at] * high, axis=0, keepdims=True)
        flux_x = flux_in[0, lev]
        flux_y = flux_in[1, lev] + (jnp.where(row == rows - 1, plus, 0.0) - jnp.where(row == 0, minus, 0.0))
        flux[0, lev] = flux_x
        flux[1, lev] = flux_y
        col_x += flux_x
        col_y += flux_y
    right, left = lane_shifts(col_x)
    down, up = row_shifts(col_y, 0.0, 0.0)
    top = depth == 0
    source = GRAVITY * (right - left + down - up)
    send[0:rows] = source + jnp.where(top, surface_cot[...], 0.0)
    send[rows : rows + 8] = jnp.where(kind == 0, col_y[0:1], jnp.where(kind == 1, col_y[rows - 1 : rows], 0.0))
    send[rows + 8 : 2 * rows + 8] = jnp.where(top, damping[...], 0.0)

    low_s, high_s = halo(levels * tracers, 8)
    low_s, high_s = ADVECT * GRAVITY * low_s[0:1], ADVECT * GRAVITY * high_s[0:1]
    for j in range(levels):
        lev = level(j, depth, levels)
        at = pl.multiple_of(lev * tracers, tracers)
        low, high = halo(at, tracers)
        first = low_s * packed[2, pl.ds(at, tracers)] + (DIFFUSE - (lines[pl.ds(lev, 1)] + low_s)) * low
        final = high_s * packed[3, pl.ds(at, tracers)] + (DIFFUSE + (lines[pl.ds(levels + lev, 1)] - high_s)) * high
        if j > 0:
            first = first + lines[2 * levels + j - 1 : 2 * levels + j] * delta[0, j - 1]
            final = final + lines[3 * levels + j - 1 : 3 * levels + j] * delta[1, j - 1]
        delta[0, j] = first
        delta[1, j] = final
    send[2 * rows + 8 : 2 * rows + 8 + tracers] = delta[0, levels - 1]
    send[2 * rows + 8 + tracers : 2 * rows + 8 + 2 * tracers] = delta[1, levels - 1]


def solve_kernel(tiles, partners, flux, mix, nums, last, delta, other_mix, other_last, swept, own, *refs):
    steps = len(partners)
    got, rest = refs[:steps], refs[steps:]
    swaps = sum(differ(pair) for pair in partners)
    swapped, rest = iter(rest[:swaps]), rest[swaps:]
    adj_tracer_out, adj_velocity, adj_surface = rest[:3]
    resid, image, moved, damp, firsts, finals, direc, sol, adj_tracer, sem = rest[3:]
    levels, rows, cols = flux.shape[1:]
    me = lax.axis_index("tile")
    depth = lax.axis_index("depth")

    tracers = last.shape[0]
    inverse, ratio, rest = chain(mix, depth)
    _, _, other_rest = chain(other_mix, 1 - depth)
    own_w, other_w = meet(rest, other_rest, mix[levels - 1], other_mix[levels - 1], depth)
    row = lax.broadcasted_iota(jnp.int32, (rows, cols), 0)
    far = 2 * rows + 8

    def with_rows(block, first, final):
        return block + (jnp.where(row == 0, first, 0.0) + jnp.where(row == rows - 1, final, 0.0))

    for tr in range(tracers):
        num = with_rows(last[tr], delta[0, levels - 1, tr : tr + 1], delta[1, levels - 1, tr : tr + 1])
        at = far + tr
        other_num = with_rows(other_last[tr], swept[at : at + 1], swept[at + tracers : at + tracers + 1])
        value = own_w * num + other_w * other_num
        adj_tracer[tr, level(levels - 1, depth, levels)] = value
        for j in range(levels - 2, -1, -1):
            num = with_rows(nums[j, tr], delta[0, j, tr : tr + 1], delta[1, j, tr : tr + 1])
            value = inverse[j] * num + ratio[j] * value
            adj_tracer[tr, level(j, depth, levels)] = value
    copy_out = pltpu.make_async_copy(adj_tracer, adj_tracer_out, sem)
    copy_out.start()

    parts = cols // 128
    lanes = [slice(128 * h, 128 * (h + 1)) for h in range(parts)]

    def place(ref, tile):
        for h, lane in enumerate(lanes):
            resid[h, pl.ds(tiles + tile, rows, stride=tiles)] = ref[0:rows, lane]
            damp[h, pl.ds(tile, rows, stride=tiles)] = 4.0 + ref[rows + 8 : 2 * rows + 8, lane]
            firsts[h, pl.ds(tile, 1)] = ref[rows : rows + 1, lane]
            finals[h, pl.ds(tile, 1)] = ref[rows + 1 : rows + 2, lane]

    place(own, me)
    for step, (for_top, for_bottom) in enumerate(partners):
        place(got[step], partner(me, jnp.where(depth == 0, for_top, for_bottom), tiles))
        if differ((for_top, for_bottom)):
            place(next(swapped), partner(me, jnp.where(depth == 0, for_bottom, for_top), tiles))

    column = lax.broadcasted_iota(jnp.int32, (tiles, 128), 1)

    def group(ref, g):
        return [ref[h, g * tiles : (g + 1) * tiles] for h in range(parts)]

    def keep(ref, g, values):
        for h, value in enumerate(values):
            ref[h, g * tiles : (g + 1) * tiles] = value

    def beside(values):
        left = [pltpu.roll(v, 1, 1) for v in values]
        right = [pltpu.roll(v, 127, 1) for v in values]
        left = [jnp.where(column == 0, left[h - 1] if h > 0 else 0.0, left[h]) for h in range(parts)]
        right = [jnp.where(column == 127, right[h + 1] if h < parts - 1 else 0.0, right[h]) for h in range(parts)]
        return [p + q for p, q in zip(left, right)]

    for h in range(parts):
        next_first, _ = row_shifts(firsts[h], 0.0, 0.0)
        _, last_final = row_shifts(finals[h], 0.0, 0.0)
        resid[h, rows * tiles : (rows + 1) * tiles] += GRAVITY * next_first
        resid[h, tiles : 2 * tiles] -= GRAVITY * last_final

    def sweep(fresh):
        final, first = fresh(rows - 1), fresh(0)
        above = [row_shifts(v, 0.0, 0.0)[1] for v in final]
        after = [row_shifts(v, 0.0, 0.0)[0] for v in first]
        keep(resid, 0, above)
        keep(resid, rows + 1, after)
        norms = [jnp.zeros((tiles, 128), F32)] * parts
        dots = [jnp.zeros((tiles, 128), F32)] * parts
        here = first
        for b in range(rows):
            below = fresh(b + 1) if b + 1 < rows - 1 else final if b + 1 == rows - 1 else after
            side, weight = beside(here), group(damp, b)
            made = [weight[h] * here[h] - ((above[h] + below[h]) + side[h]) for h in range(parts)]
            keep(image, b, made)
            norms = [norms[h] + here[h] * here[h] for h in range(parts)]
            dots = [dots[h] + here[h] * made[h] for h in range(parts)]
            above, here = here, below
        return jnp.sum(sum(norms), keepdims=True), jnp.sum(sum(dots), keepdims=True)

    def step_own(alpha, beta):
        for h in range(parts):
            d = resid[h, pl.ds(me, rows + 2, stride=tiles)] + beta * direc[h]
            direc[h] = d
            sol[h] += alpha * d

    direc[...] = jnp.zeros_like(direc)
    sol[...] = jnp.zeros_like(sol)
    moved[...] = jnp.zeros_like(moved)
    norm, dot = sweep(lambda b: group(resid, b + 1))

    def advance(turn, carry):
        over_norm, inv, alpha, beta = carry
        step_own(alpha, beta)

        def fresh(b):
            old, made, kept = group(resid, b + 1), group(image, b), group(moved, b)
            kept = [made[h] + beta * kept[h] for h in range(parts)]
            new = [old[h] - alpha * kept[h] for h in range(parts)]
            keep(moved, b, kept)
            keep(resid, b + 1, new)
            return new

        norm, dot = sweep(fresh)
        beta = norm * over_norm
        divisor = dot - norm * (beta * inv)
        over_norm = 1.0 / norm
        return over_norm, divisor * over_norm, norm / divisor, beta

    over_norm = 1.0 / norm
    first = (over_norm, dot * over_norm, norm / dot, jnp.zeros_like(norm))
    _, _, alpha, beta = lax.fori_loop(0, ITERS - 1, advance, first)
    step_own(alpha, beta)

    x = jnp.concatenate([sol[h, 1 : rows + 1] for h in range(parts)], axis=1)
    adj_surface[...] = x
    right, left = lane_shifts(x)
    slope_x = ADVECT * (right - left)
    slope_y = jnp.concatenate([ADVECT * (sol[h, 2 : rows + 2] - sol[h, 0:rows]) for h in range(parts)], axis=1)
    for lev in range(levels):
        adj_velocity[0, lev] = flux[0, lev] + slope_x
        adj_velocity[1, lev] = flux[1, lev] + slope_y
    copy_out.wait()


def solve_call(partners, args, tiles):
    flux, last = args[0], args[3]
    tracers = last.shape[0]
    levels, rows, cols = flux.shape[1:]
    plane, height, parts = (rows, cols), tiles * rows, cols // 128
    block = (tracers, levels) + plane
    return call(
        functools.partial(solve_kernel, tiles, partners),
        [block, (2, levels) + plane, plane],
        args,
        scratch=[
            pltpu.VMEM((parts, height + 2 * tiles, 128), F32),
            pltpu.VMEM((parts, height, 128), F32),
            pltpu.VMEM((parts, height, 128), F32),
            pltpu.VMEM((parts, height, 128), F32),
            pltpu.VMEM((parts, tiles, 128), F32),
            pltpu.VMEM((parts, tiles, 128), F32),
            pltpu.VMEM((parts, rows + 2, 128), F32),
            pltpu.VMEM((parts, rows + 2, 128), F32),
            pltpu.VMEM(block, F32),
            pltpu.SemaphoreType.DMA(()),
        ],
        hbm_out=(0,),
    )


def partner(tile, offset, tiles):
    if tiles & (tiles - 1) == 0:
        return tile ^ offset
    return (offset + tiles - tile) % tiles


def differ(pair):
    return pair[0] != pair[1]


def partner_offsets(tiles):
    if tiles & (tiles - 1) == 0:
        others = sorted(range(1, tiles), key=lambda k: (bin(k).count("1"), k))
    else:
        others = list(range(tiles))
    if len(others) % 2 == 1:
        others = others[:1] + others
    return [(others[i], others[i + 1]) for i in range(0, len(others), 2)]


def body(tracer_start, velocity, surface, mixing, land_mask, damping, tracer_cot, surface_cot):
    tracers, levels, rows, cols = tracer_start.shape
    tiles = lax.axis_size("tile")
    swap = [(0, 1), (1, 0)]
    plane = (rows, cols)
    block = (tracers, levels) + plane
    edge = (tracers * levels + 8, cols)
    edge_b, edge_a = call(
        edge_kernel,
        [edge, edge],
        [tracer_cot.reshape(tracers * levels, rows, cols), land_mask, surface, tracer_start, mixing, velocity],
        scratch=[
            pltpu.VMEM((2, tracers * levels, 8, cols), F32),
            pltpu.VMEM((2, levels, 8, cols), jnp.int32),
            pltpu.VMEM((2, 8, cols), F32),
            pltpu.SemaphoreType.DMA((6,)),
        ],
        hbm_in=range(6),
        near=True,
    )
    pairs_a = [(i, i + 1) for i in range(0, tiles - 1, 2)]
    pairs_b = [(i, i + 1) for i in range(1, tiles - 1, 2)]
    other = lax.ppermute(tracer_start, "depth", swap)
    other_mix = lax.ppermute(mixing, "depth", swap)
    edge_b = lax.ppermute(edge_b, "tile", pairs_b + [(b, a) for a, b in pairs_b])
    edge_a = lax.ppermute(edge_a, "tile", pairs_a + [(b, a) for a, b in pairs_a])
    planes = tracers * levels
    flux, nums, last, packed, lines = call(
        interior_kernel,
        [(2, levels) + plane, (levels - 1, tracers) + plane, (tracers,) + plane, (4, planes, cols), (4 * levels, cols)],
        [tracer_start, mixing, tracer_cot, land_mask, velocity, surface, other, other_mix],
        scratch=[pltpu.VMEM((2, levels) + plane, F32)],
    )
    flux, delta, part = call(
        column_kernel,
        [(2, levels) + plane, (2, levels, tracers, cols), (2 * rows + 8 + 2 * tracers, cols)],
        [flux, packed, lines, edge_b, edge_a, surface_cot, damping],
    )
    swept = lax.ppermute(part, "depth", swap)
    own = part[: 2 * rows + 8] + swept[: 2 * rows + 8]

    partners = partner_offsets(tiles)
    got = []
    for for_top, for_bottom in partners:
        pairs = [(2 * partner(t, for_top, tiles), 2 * t) for t in range(tiles)]
        pairs += [(2 * partner(t, for_bottom, tiles) + 1, 2 * t + 1) for t in range(tiles)]
        got.append(lax.ppermute(own, ("tile", "depth"), pairs))
    swapped = [lax.ppermute(piece, "depth", swap) for piece, pair in zip(got, partners) if differ(pair)]

    last_late, _ = lax.optimization_barrier((last, own))
    other_last = lax.ppermute(last_late, "depth", swap)
    return solve_call(
        partners,
        [flux, mixing, nums, last, delta, other_mix, other_last, swept, own] + got + swapped,
        tiles,
    )


def solution(mesh):
    return jax.shard_map(
        body,
        mesh=mesh,
        in_specs=(
            P("grp", "depth", "tile", None),
            P("grp", "depth", "tile", None),
            P(("grp", "tile"), None),
            P(("grp", "depth"), "tile", None),
            P("depth", "tile", None),
            P("tile", None),
            P("grp", "depth", "tile", None),
            P(("grp", "tile"), None),
        ),
        out_specs=(
            P("grp", "depth", "tile", None),
            P("grp", "depth", "tile", None),
            P(("grp", "tile"), None),
        ),
        check_vma=False,
    )
```

```python
import functools

import jax
import jax.numpy as jnp
from jax import lax
from jax.experimental import pallas as pl
from jax.experimental.pallas import tpu as pltpu
from jax.sharding import PartitionSpec as P

ITERS = 6
ADVECT = 0.25
DIFFUSE = 0.1
GRAVITY = 0.5

F32 = jnp.float32
VMEM = pl.BlockSpec(memory_space=pltpu.VMEM)
HBM = pl.BlockSpec(memory_space=pltpu.HBM)


def call(kernel, outs, args, scratch=(), flops=2_000_000, hbm_in=(), hbm_out=(), near=False):
    nbytes = sum(a.size * 4 for a in args) + sum(4 * functools.reduce(lambda p, q: p * q, s) for s in outs)
    if near:
        args = [pltpu.with_memory_space_constraint(a, pltpu.HBM) for a in args]
    return pl.pallas_call(
        kernel,
        out_shape=[pltpu.VMEM(s, F32) if near else jax.ShapeDtypeStruct(s, F32) for s in outs],
        in_specs=[HBM if i in hbm_in else VMEM for i in range(len(args))],
        out_specs=[HBM if i in hbm_out else VMEM for i in range(len(outs))],
        scratch_shapes=list(scratch),
        cost_estimate=pl.CostEstimate(flops=flops, bytes_accessed=nbytes, transcendentals=0),
        compiler_params=pltpu.CompilerParams(vmem_limit_bytes=40 * 1024 * 1024),
    )(*args)


def lane_shifts(f):
    lane = lax.broadcasted_iota(jnp.int32, f.shape, f.ndim - 1)
    cols = f.shape[-1]
    after = jnp.where(lane == cols - 1, 0.0, pltpu.roll(f, cols - 1, f.ndim - 1))
    before = jnp.where(lane == 0, 0.0, pltpu.roll(f, 1, f.ndim - 1))
    return after, before


def row_shifts(f, low, high):
    row = lax.broadcasted_iota(jnp.int32, f.shape, 0)
    rows = f.shape[0]
    after = jnp.where(row == rows - 1, high, pltpu.roll(f, rows - 1, 0))
    before = jnp.where(row == 0, low, pltpu.roll(f, 1, 0))
    return after, before


def chain(mix_ref, depth):
    levels = mix_ref.shape[0]
    links = [mix_ref[j + depth * (levels - 2 - 2 * j)] for j in range(levels - 1)]
    rest = jnp.ones_like(links[0])
    inverse, ratio = [], []
    for link in links:
        inv = 1.0 / (rest + link)
        inverse.append(inv)
        ratio.append(link * inv)
        rest = 1.0 + link * (rest * inv)
    return inverse, ratio, rest


def level(j, depth, levels):
    return j + depth * (levels - 1 - 2 * j)


def meet(rest, other_rest, own_mix, other_mix, depth):
    link = jnp.where(depth == 0, own_mix, other_mix)
    det = rest * other_rest + link * (rest + other_rest)
    inv = 1.0 / det
    return (other_rest + link) * inv, link * inv


def edge_kernel(cot_in, mask_in, surface_in, tracer_in, mix_in, velocity_in, edge_b, edge_a, cot, mask, surface, sems):
    levels, rows, _ = mask_in.shape
    tracers = cot_in.shape[0] // levels
    odd = lax.rem(lax.axis_index("tile"), 2) == 1
    copies = []
    for side, start in enumerate((0, rows - 8)):
        part = pl.ds(start, 8)
        moves = [(cot_in.at[:, part], cot), (mask_in.at[:, part], mask), (surface_in.at[part], surface)]
        for src, dst in moves:
            copies.append(pltpu.make_async_copy(src, dst.at[side], sems.at[len(copies)]))
    for copy in copies:
        copy.start()
    for copy in copies:
        copy.wait()
    for lev in range(levels):
        first_wet = mask[0, lev, 0:1].astype(F32)
        last_wet = mask[1, lev, 7:8].astype(F32)
        for tr in range(tracers):
            first = cot[0, tr * levels + lev, 0:1] * first_wet
            last = cot[1, tr * levels + lev, 7:8] * last_wet
            at = lev * tracers + tr
            edge_a[at : at + 1] = jnp.where(odd, first, last)
            edge_b[at : at + 1] = jnp.where(odd, last, first)
    at = tracers * levels
    edge_a[at : at + 8] = jnp.zeros_like(edge_a[at : at + 8])
    edge_b[at : at + 8] = jnp.zeros_like(edge_b[at : at + 8])
    first, last = surface[0, 0:1], surface[1, 7:8]
    edge_a[at : at + 1] = jnp.where(odd, first, last)
    edge_b[at : at + 1] = jnp.where(odd, last, first)


def interior_kernel(tracer, mix, cot, mask, velocity, surface, other, other_mix, flux, nums, last, packed, lines, speed):
    tracers, levels, rows, cols = tracer.shape
    depth = lax.axis_index("depth")
    inverse, ratio, rest = chain(mix, depth)
    _, other_ratio, other_rest = chain(other_mix, 1 - depth)
    own_w, other_w = meet(rest, other_rest, mix[levels - 1], other_mix[levels - 1], depth)
    right, left = lane_shifts(surface[...])
    down, up = row_shifts(surface[...], 0.0, 0.0)
    for lev in range(levels):
        speed[0, lev] = ADVECT * (velocity[0, lev] - GRAVITY * (right - left))
        along = ADVECT * (velocity[1, lev] - GRAVITY * (down - up))
        speed[1, lev] = along
        lines[lev : lev + 1] = along[0:1]
        lines[levels + lev : levels + lev + 1] = along[rows - 1 : rows]
    lines[2 * levels : 4 * levels] = jnp.zeros((2 * levels, cols), F32)
    for j in range(levels - 1):
        at = 2 * levels + j
        lines[at : at + 1] = ratio[j][0:1]
        lines[at + levels : at + levels + 1] = ratio[j][rows - 1 : rows]
    flux[...] = jnp.zeros_like(flux)
    for tr in range(tracers):
        held = [tracer[tr, level(0, depth, levels)]]
        for j in range(1, levels):
            held.append(tracer[tr, level(j, depth, levels)] + ratio[j - 1] * held[-1])
        met = other[tr, level(0, 1 - depth, levels)]
        for j in range(1, levels):
            met = other[tr, level(j, 1 - depth, levels)] + other_ratio[j - 1] * met
        value = own_w * held[-1] + other_w * met
        outs = [None] * levels
        for j in range(levels - 1, -1, -1):
            lev = level(j, depth, levels)
            if j < levels - 1:
                value = inverse[j] * held[j] + ratio[j] * value
            block = cot[tr, lev] * mask[lev].astype(F32)
            right, left = lane_shifts(block)
            down, up = row_shifts(block, 0.0, 0.0)
            across, along = right - left, down - up
            flux[0, lev] += ADVECT * (value * across)
            flux[1, lev] += ADVECT * (value * along)
            outs[j] = (
                block
                + (speed[0, lev] * across + speed[1, lev] * along)
                + DIFFUSE * (down + up + right + left - 4.0 * block)
            )
            at = lev * tracers + tr
            packed[0, pl.ds(at, 1)] = value[0:1]
            packed[1, pl.ds(at, 1)] = value[rows - 1 : rows]
            packed[2, pl.ds(at, 1)] = block[1:2]
            packed[3, pl.ds(at, 1)] = block[rows - 2 : rows - 1]
        num = outs[0]
        for j in range(1, levels):
            nums[j - 1, tr] = num
            num = outs[j] + ratio[j - 1] * num
        last[tr] = num


def column_kernel(flux_in, packed, lines, edge_b, edge_a, surface_cot, damping, flux, delta, send):
    levels, rows, cols = flux.shape[1:]
    tracers = delta.shape[2]
    depth = lax.axis_index("depth")
    odd = lax.rem(lax.axis_index("tile"), 2) == 1
    row = lax.broadcasted_iota(jnp.int32, (rows, cols), 0)

    def halo(at, size):
        from_a, from_b = edge_a[pl.ds(at, size)], edge_b[pl.ds(at, size)]
        return jnp.where(odd, from_a, from_b), jnp.where(odd, from_b, from_a)

    col_x = jnp.zeros((rows, cols), F32)
    col_y = jnp.zeros((rows, cols), F32)
    for lev in range(levels):
        low, high = halo(lev * tracers, tracers)
        at = slice(lev * tracers, (lev + 1) * tracers)
        minus = ADVECT * jnp.sum(packed[0, at] * low, axis=0, keepdims=True)
        plus = ADVECT * jnp.sum(packed[1, at] * high, axis=0, keepdims=True)
        flux_x = flux_in[0, lev]
        flux_y = flux_in[1, lev] + (jnp.where(row == rows - 1, plus, 0.0) - jnp.where(row == 0, minus, 0.0))
        flux[0, lev] = flux_x
        flux[1, lev] = flux_y
        col_x += flux_x
        col_y += flux_y
    right, left = lane_shifts(col_x)
    down, up = row_shifts(col_y, 0.0, 0.0)
    top = depth == 0
    source = GRAVITY * (right - left + down - up)
    source = source + jnp.where(top, surface_cot[...], 0.0)
    weight = jnp.where(top, damping[...], 0.0)
    parts = cols // 128
    for h in range(parts):
        lane = slice(128 * h, 128 * (h + 1))
        send[h * rows : (h + 1) * rows] = source[:, lane]
        send[(parts + h) * rows : (parts + h + 1) * rows] = weight[:, lane]
    at = 2 * parts * rows
    kind = lax.broadcasted_iota(jnp.int32, (8, 128), 0)
    ends = jnp.zeros((8, 128), F32)
    for h in range(parts):
        lane = slice(128 * h, 128 * (h + 1))
        ends = jnp.where(kind == h, col_y[0:1, lane], ends)
        ends = jnp.where(kind == parts + h, col_y[rows - 1 : rows, lane], ends)
    send[at : at + 8] = ends

    low_s, high_s = halo(levels * tracers, 8)
    low_s, high_s = ADVECT * GRAVITY * low_s[0:1], ADVECT * GRAVITY * high_s[0:1]
    for j in range(levels):
        lev = level(j, depth, levels)
        at = pl.multiple_of(lev * tracers, tracers)
        low, high = halo(at, tracers)
        first = low_s * packed[2, pl.ds(at, tracers)] + (DIFFUSE - (lines[pl.ds(lev, 1)] + low_s)) * low
        final = high_s * packed[3, pl.ds(at, tracers)] + (DIFFUSE + (lines[pl.ds(levels + lev, 1)] - high_s)) * high
        if j > 0:
            first = first + lines[2 * levels + j - 1 : 2 * levels + j] * delta[0, j - 1]
            final = final + lines[3 * levels + j - 1 : 3 * levels + j] * delta[1, j - 1]
        delta[0, j] = first
        delta[1, j] = final
    at = 2 * parts * rows + 8
    for side in range(2):
        for h in range(parts):
            send[at : at + tracers] = delta[side, levels - 1, :, 128 * h : 128 * (h + 1)]
            at += tracers


def solve_kernel(tiles, partners, flux, mix, nums, last, delta, other_mix, other_last, swept, own, *refs):
    steps = len(partners)
    got, rest = refs[:steps], refs[steps:]
    swaps = sum(differ(pair) for pair in partners)
    swapped, rest = iter(rest[:swaps]), rest[swaps:]
    adj_tracer_out, adj_velocity, adj_surface = rest[:3]
    resid, image, moved, damp, firsts, finals, direc, sol, adj_tracer, sem = rest[3:]
    levels, rows, cols = flux.shape[1:]
    me = lax.axis_index("tile")
    depth = lax.axis_index("depth")

    tracers = last.shape[0]
    inverse, ratio, rest = chain(mix, depth)
    _, _, other_rest = chain(other_mix, 1 - depth)
    own_w, other_w = meet(rest, other_rest, mix[levels - 1], other_mix[levels - 1], depth)
    row = lax.broadcasted_iota(jnp.int32, (rows, cols), 0)
    parts = cols // 128
    far = 2 * parts * rows + 8

    def with_rows(block, first, final):
        return block + (jnp.where(row == 0, first, 0.0) + jnp.where(row == rows - 1, final, 0.0))

    for tr in range(tracers):
        num = with_rows(last[tr], delta[0, levels - 1, tr : tr + 1], delta[1, levels - 1, tr : tr + 1])
        first, final = [
            jnp.concatenate([swept[at + h * tracers : at + h * tracers + 1] for h in range(parts)], axis=1)
            for at in (far + tr, far + parts * tracers + tr)
        ]
        other_num = with_rows(other_last[tr], first, final)
        value = own_w * num + other_w * other_num
        adj_tracer[tr, level(levels - 1, depth, levels)] = value
        for j in range(levels - 2, -1, -1):
            num = with_rows(nums[j, tr], delta[0, j, tr : tr + 1], delta[1, j, tr : tr + 1])
            value = inverse[j] * num + ratio[j] * value
            adj_tracer[tr, level(j, depth, levels)] = value
    copy_out = pltpu.make_async_copy(adj_tracer, adj_tracer_out, sem)
    copy_out.start()

    ends = 2 * parts * rows

    def place(ref, tile):
        for h in range(parts):
            resid[h, pl.ds(tiles + tile, rows, stride=tiles)] = ref[h * rows : (h + 1) * rows]
            damp[h, pl.ds(tile, rows, stride=tiles)] = 4.0 + ref[(parts + h) * rows : (parts + h + 1) * rows]
            firsts[h, pl.ds(tile, 1)] = ref[ends + h : ends + h + 1]
            finals[h, pl.ds(tile, 1)] = ref[ends + parts + h : ends + parts + h + 1]

    place(own, me)
    for step, (for_top, for_bottom) in enumerate(partners):
        place(got[step], partner(me, jnp.where(depth == 0, for_top, for_bottom), tiles))
        if differ((for_top, for_bottom)):
            place(next(swapped), partner(me, jnp.where(depth == 0, for_bottom, for_top), tiles))

    column = lax.broadcasted_iota(jnp.int32, (tiles, 128), 1)

    def group(ref, g):
        return [ref[h, g * tiles : (g + 1) * tiles] for h in range(parts)]

    def keep(ref, g, values):
        for h, value in enumerate(values):
            ref[h, g * tiles : (g + 1) * tiles] = value

    def beside(values):
        left = [pltpu.roll(v, 1, 1) for v in values]
        right = [pltpu.roll(v, 127, 1) for v in values]
        left = [jnp.where(column == 0, left[h - 1] if h > 0 else 0.0, left[h]) for h in range(parts)]
        right = [jnp.where(column == 127, right[h + 1] if h < parts - 1 else 0.0, right[h]) for h in range(parts)]
        return [p + q for p, q in zip(left, right)]

    for h in range(parts):
        next_first, _ = row_shifts(firsts[h], 0.0, 0.0)
        _, last_final = row_shifts(finals[h], 0.0, 0.0)
        resid[h, rows * tiles : (rows + 1) * tiles] += GRAVITY * next_first
        resid[h, tiles : 2 * tiles] -= GRAVITY * last_final

    def sweep(fresh):
        final, first = fresh(rows - 1), fresh(0)
        above = [row_shifts(v, 0.0, 0.0)[1] for v in final]
        after = [row_shifts(v, 0.0, 0.0)[0] for v in first]
        keep(resid, 0, above)
        keep(resid, rows + 1, after)
        norms = [jnp.zeros((tiles, 128), F32)] * parts
        dots = [jnp.zeros((tiles, 128), F32)] * parts
        here = first
        for b in range(rows):
            below = fresh(b + 1) if b + 1 < rows - 1 else final if b + 1 == rows - 1 else after
            side, weight = beside(here), group(damp, b)
            made = [weight[h] * here[h] - ((above[h] + below[h]) + side[h]) for h in range(parts)]
            keep(image, b, made)
            norms = [norms[h] + here[h] * here[h] for h in range(parts)]
            dots = [dots[h] + here[h] * made[h] for h in range(parts)]
            above, here = here, below
        return jnp.sum(sum(norms), keepdims=True), jnp.sum(sum(dots), keepdims=True)

    def step_own(alpha, beta):
        for h in range(parts):
            d = resid[h, pl.ds(me, rows + 2, stride=tiles)] + beta * direc[h]
            direc[h] = d
            sol[h] += alpha * d

    direc[...] = jnp.zeros_like(direc)
    sol[...] = jnp.zeros_like(sol)
    moved[...] = jnp.zeros_like(moved)
    norm, dot = sweep(lambda b: group(resid, b + 1))

    def advance(turn, carry):
        over_norm, inv, alpha, beta = carry
        step_own(alpha, beta)

        def fresh(b):
            old, made, kept = group(resid, b + 1), group(image, b), group(moved, b)
            kept = [made[h] + beta * kept[h] for h in range(parts)]
            new = [old[h] - alpha * kept[h] for h in range(parts)]
            keep(moved, b, kept)
            keep(resid, b + 1, new)
            return new

        norm, dot = sweep(fresh)
        beta = norm * over_norm
        divisor = dot - norm * (beta * inv)
        over_norm = 1.0 / norm
        return over_norm, divisor * over_norm, norm / divisor, beta

    over_norm = 1.0 / norm
    first = (over_norm, dot * over_norm, norm / dot, jnp.zeros_like(norm))
    _, _, alpha, beta = lax.fori_loop(0, ITERS - 1, advance, first)
    step_own(alpha, beta)

    x = jnp.concatenate([sol[h, 1 : rows + 1] for h in range(parts)], axis=1)
    adj_surface[...] = x
    right, left = lane_shifts(x)
    slope_x = ADVECT * (right - left)
    slope_y = jnp.concatenate([ADVECT * (sol[h, 2 : rows + 2] - sol[h, 0:rows]) for h in range(parts)], axis=1)
    for lev in range(levels):
        adj_velocity[0, lev] = flux[0, lev] + slope_x
        adj_velocity[1, lev] = flux[1, lev] + slope_y
    copy_out.wait()


def solve_call(partners, args, tiles):
    flux, last = args[0], args[3]
    tracers = last.shape[0]
    levels, rows, cols = flux.shape[1:]
    plane, height, parts = (rows, cols), tiles * rows, cols // 128
    block = (tracers, levels) + plane
    return call(
        functools.partial(solve_kernel, tiles, partners),
        [block, (2, levels) + plane, plane],
        args,
        scratch=[
            pltpu.VMEM((parts, height + 2 * tiles, 128), F32),
            pltpu.VMEM((parts, height, 128), F32),
            pltpu.VMEM((parts, height, 128), F32),
            pltpu.VMEM((parts, height, 128), F32),
            pltpu.VMEM((parts, tiles, 128), F32),
            pltpu.VMEM((parts, tiles, 128), F32),
            pltpu.VMEM((parts, rows + 2, 128), F32),
            pltpu.VMEM((parts, rows + 2, 128), F32),
            pltpu.VMEM(block, F32),
            pltpu.SemaphoreType.DMA(()),
        ],
        hbm_out=(0,),
    )


def partner(tile, offset, tiles):
    if tiles & (tiles - 1) == 0:
        return tile ^ offset
    return (offset + tiles - tile) % tiles


def differ(pair):
    return pair[0] != pair[1]


def partner_offsets(tiles):
    if tiles & (tiles - 1) == 0:
        others = sorted(range(1, tiles), key=lambda k: (bin(k).count("1"), k))
    else:
        others = list(range(tiles))
    if len(others) % 2 == 1:
        others = others[:1] + others
    return [(others[i], others[i + 1]) for i in range(0, len(others), 2)]


def body(tracer_start, velocity, surface, mixing, land_mask, damping, tracer_cot, surface_cot):
    tracers, levels, rows, cols = tracer_start.shape
    tiles = lax.axis_size("tile")
    swap = [(0, 1), (1, 0)]
    plane = (rows, cols)
    block = (tracers, levels) + plane
    edge = (tracers * levels + 8, cols)
    edge_b, edge_a = call(
        edge_kernel,
        [edge, edge],
        [tracer_cot.reshape(tracers * levels, rows, cols), land_mask, surface, tracer_start, mixing, velocity],
        scratch=[
            pltpu.VMEM((2, tracers * levels, 8, cols), F32),
            pltpu.VMEM((2, levels, 8, cols), jnp.int32),
            pltpu.VMEM((2, 8, cols), F32),
            pltpu.SemaphoreType.DMA((6,)),
        ],
        hbm_in=range(6),
        near=True,
    )
    pairs_a = [(i, i + 1) for i in range(0, tiles - 1, 2)]
    pairs_b = [(i, i + 1) for i in range(1, tiles - 1, 2)]
    other = lax.ppermute(tracer_start, "depth", swap)
    other_mix = lax.ppermute(mixing, "depth", swap)
    edge_b = lax.ppermute(edge_b, "tile", pairs_b + [(b, a) for a, b in pairs_b])
    edge_a = lax.ppermute(edge_a, "tile", pairs_a + [(b, a) for a, b in pairs_a])
    planes, parts = tracers * levels, cols // 128
    share = 2 * parts * rows + 8
    flux, nums, last, packed, lines = call(
        interior_kernel,
        [(2, levels) + plane, (levels - 1, tracers) + plane, (tracers,) + plane, (4, planes, cols), (4 * levels, cols)],
        [tracer_start, mixing, tracer_cot, land_mask, velocity, surface, other, other_mix],
        scratch=[pltpu.VMEM((2, levels) + plane, F32)],
    )
    flux, delta, part = call(
        column_kernel,
        [(2, levels) + plane, (2, levels, tracers, cols), (share + 2 * parts * tracers, 128)],
        [flux, packed, lines, edge_b, edge_a, surface_cot, damping],
    )
    swept = lax.ppermute(part, "depth", swap)
    own = part[:share] + swept[:share]

    partners = partner_offsets(tiles)
    got = []
    for for_top, for_bottom in partners:
        pairs = [(2 * partner(t, for_top, tiles), 2 * t) for t in range(tiles)]
        pairs += [(2 * partner(t, for_bottom, tiles) + 1, 2 * t + 1) for t in range(tiles)]
        got.append(lax.ppermute(own, ("tile", "depth"), pairs))
    swapped = [lax.ppermute(piece, "depth", swap) for piece, pair in zip(got, partners) if differ(pair)]

    last_late, _ = lax.optimization_barrier((last, own))
    other_last = lax.ppermute(last_late, "depth", swap)
    return solve_call(
        partners,
        [flux, mixing, nums, last, delta, other_mix, other_last, swept, own] + got + swapped,
        tiles,
    )


def solution(mesh):
    return jax.shard_map(
        body,
        mesh=mesh,
        in_specs=(
            P("grp", "depth", "tile", None),
            P("grp", "depth", "tile", None),
            P(("grp", "tile"), None),
            P(("grp", "depth"), "tile", None),
            P("depth", "tile", None),
            P("tile", None),
            P("grp", "depth", "tile", None),
            P(("grp", "tile"), None),
        ),
        out_specs=(
            P("grp", "depth", "tile", None),
            P("grp", "depth", "tile", None),
            P(("grp", "tile"), None),
        ),
        check_vma=False,
    )
```

```python
import functools

import jax
import jax.numpy as jnp
from jax import lax
from jax.experimental import pallas as pl
from jax.experimental.pallas import tpu as pltpu
from jax.sharding import PartitionSpec as P

ITERS = 6
ADVECT = 0.25
DIFFUSE = 0.1
GRAVITY = 0.5

F32 = jnp.float32
VMEM = pl.BlockSpec(memory_space=pltpu.VMEM)
HBM = pl.BlockSpec(memory_space=pltpu.HBM)


def call(kernel, outs, args, scratch=(), flops=2_000_000, hbm_in=(), hbm_out=(), near=False):
    nbytes = sum(a.size * 4 for a in args) + sum(4 * functools.reduce(lambda p, q: p * q, s) for s in outs)
    if near:
        args = [pltpu.with_memory_space_constraint(a, pltpu.HBM) for a in args]
    return pl.pallas_call(
        kernel,
        out_shape=[pltpu.VMEM(s, F32) if near else jax.ShapeDtypeStruct(s, F32) for s in outs],
        in_specs=[HBM if i in hbm_in else VMEM for i in range(len(args))],
        out_specs=[HBM if i in hbm_out else VMEM for i in range(len(outs))],
        scratch_shapes=list(scratch),
        cost_estimate=pl.CostEstimate(flops=flops, bytes_accessed=nbytes, transcendentals=0),
        compiler_params=pltpu.CompilerParams(vmem_limit_bytes=40 * 1024 * 1024),
    )(*args)


def lane_shifts(f):
    lane = lax.broadcasted_iota(jnp.int32, f.shape, f.ndim - 1)
    cols = f.shape[-1]
    after = jnp.where(lane == cols - 1, 0.0, pltpu.roll(f, cols - 1, f.ndim - 1))
    before = jnp.where(lane == 0, 0.0, pltpu.roll(f, 1, f.ndim - 1))
    return after, before


def row_shifts(f, low, high):
    row = lax.broadcasted_iota(jnp.int32, f.shape, 0)
    rows = f.shape[0]
    after = jnp.where(row == rows - 1, high, pltpu.roll(f, rows - 1, 0))
    before = jnp.where(row == 0, low, pltpu.roll(f, 1, 0))
    return after, before


def chain(mix_ref, depth):
    levels = mix_ref.shape[0]
    links = [mix_ref[j + depth * (levels - 2 - 2 * j)] for j in range(levels - 1)]
    rest = jnp.ones_like(links[0])
    inverse, ratio = [], []
    for link in links:
        inv = 1.0 / (rest + link)
        inverse.append(inv)
        ratio.append(link * inv)
        rest = 1.0 + link * (rest * inv)
    return inverse, ratio, rest


def level(j, depth, levels):
    return j + depth * (levels - 1 - 2 * j)


def meet(rest, other_rest, own_mix, other_mix, depth):
    link = jnp.where(depth == 0, own_mix, other_mix)
    det = rest * other_rest + link * (rest + other_rest)
    inv = 1.0 / det
    return (other_rest + link) * inv, link * inv


def edge_kernel(cot_in, mask_in, surface_in, tracer_in, mix_in, velocity_in, edge_b, edge_a, cot, mask, surface, sems):
    levels, rows, _ = mask_in.shape
    tracers = cot_in.shape[0] // levels
    odd = lax.rem(lax.axis_index("tile"), 2) == 1
    copies = []
    for side, start in enumerate((0, rows - 8)):
        part = pl.ds(start, 8)
        moves = [(cot_in.at[:, part], cot), (mask_in.at[:, part], mask), (surface_in.at[part], surface)]
        for src, dst in moves:
            copies.append(pltpu.make_async_copy(src, dst.at[side], sems.at[len(copies)]))
    for copy in copies:
        copy.start()
    for copy in copies:
        copy.wait()
    for lev in range(levels):
        first_wet = mask[0, lev, 0:1].astype(F32)
        last_wet = mask[1, lev, 7:8].astype(F32)
        for tr in range(tracers):
            first = cot[0, tr * levels + lev, 0:1] * first_wet
            last = cot[1, tr * levels + lev, 7:8] * last_wet
            at = lev * tracers + tr
            edge_a[at : at + 1] = jnp.where(odd, first, last)
            edge_b[at : at + 1] = jnp.where(odd, last, first)
    at = tracers * levels
    edge_a[at : at + 8] = jnp.zeros_like(edge_a[at : at + 8])
    edge_b[at : at + 8] = jnp.zeros_like(edge_b[at : at + 8])
    first, last = surface[0, 0:1], surface[1, 7:8]
    edge_a[at : at + 1] = jnp.where(odd, first, last)
    edge_b[at : at + 1] = jnp.where(odd, last, first)


def interior_kernel(tracer, mix, cot, mask, velocity, surface, other, other_mix, flux, nums, last, packed, lines, speed):
    tracers, levels, rows, cols = tracer.shape
    depth = lax.axis_index("depth")
    inverse, ratio, rest = chain(mix, depth)
    _, other_ratio, other_rest = chain(other_mix, 1 - depth)
    own_w, other_w = meet(rest, other_rest, mix[levels - 1], other_mix[levels - 1], depth)
    right, left = lane_shifts(surface[...])
    down, up = row_shifts(surface[...], 0.0, 0.0)
    for lev in range(levels):
        speed[0, lev] = ADVECT * (velocity[0, lev] - GRAVITY * (right - left))
        along = ADVECT * (velocity[1, lev] - GRAVITY * (down - up))
        speed[1, lev] = along
        lines[lev : lev + 1] = along[0:1]
        lines[levels + lev : levels + lev + 1] = along[rows - 1 : rows]
    lines[2 * levels : 4 * levels] = jnp.zeros((2 * levels, cols), F32)
    for j in range(levels - 1):
        at = 2 * levels + j
        lines[at : at + 1] = ratio[j][0:1]
        lines[at + levels : at + levels + 1] = ratio[j][rows - 1 : rows]
    flux[...] = jnp.zeros_like(flux)
    for tr in range(tracers):
        held = [tracer[tr, level(0, depth, levels)]]
        for j in range(1, levels):
            held.append(tracer[tr, level(j, depth, levels)] + ratio[j - 1] * held[-1])
        met = other[tr, level(0, 1 - depth, levels)]
        for j in range(1, levels):
            met = other[tr, level(j, 1 - depth, levels)] + other_ratio[j - 1] * met
        value = own_w * held[-1] + other_w * met
        outs = [None] * levels
        for j in range(levels - 1, -1, -1):
            lev = level(j, depth, levels)
            if j < levels - 1:
                value = inverse[j] * held[j] + ratio[j] * value
            block = cot[tr, lev] * mask[lev].astype(F32)
            right, left = lane_shifts(block)
            down, up = row_shifts(block, 0.0, 0.0)
            across, along = right - left, down - up
            flux[0, lev] += ADVECT * (value * across)
            flux[1, lev] += ADVECT * (value * along)
            outs[j] = (
                block
                + (speed[0, lev] * across + speed[1, lev] * along)
                + DIFFUSE * (down + up + right + left - 4.0 * block)
            )
            at = lev * tracers + tr
            packed[0, pl.ds(at, 1)] = value[0:1]
            packed[1, pl.ds(at, 1)] = value[rows - 1 : rows]
            packed[2, pl.ds(at, 1)] = block[1:2]
            packed[3, pl.ds(at, 1)] = block[rows - 2 : rows - 1]
        num = outs[0]
        for j in range(1, levels):
            nums[j - 1, tr] = num
            num = outs[j] + ratio[j - 1] * num
        last[tr] = num


def column_kernel(flux_in, packed, lines, edge_b, edge_a, surface_cot, damping, flux, delta, send):
    levels, rows, cols = flux.shape[1:]
    tracers = delta.shape[2]
    depth = lax.axis_index("depth")
    odd = lax.rem(lax.axis_index("tile"), 2) == 1
    row = lax.broadcasted_iota(jnp.int32, (rows, cols), 0)

    def halo(at, size):
        from_a, from_b = edge_a[pl.ds(at, size)], edge_b[pl.ds(at, size)]
        return jnp.where(odd, from_a, from_b), jnp.where(odd, from_b, from_a)

    col_x = jnp.zeros((rows, cols), F32)
    col_y = jnp.zeros((rows, cols), F32)
    for lev in range(levels):
        low, high = halo(lev * tracers, tracers)
        at = slice(lev * tracers, (lev + 1) * tracers)
        minus = ADVECT * jnp.sum(packed[0, at] * low, axis=0, keepdims=True)
        plus = ADVECT * jnp.sum(packed[1, at] * high, axis=0, keepdims=True)
        flux_x = flux_in[0, lev]
        flux_y = flux_in[1, lev] + (jnp.where(row == rows - 1, plus, 0.0) - jnp.where(row == 0, minus, 0.0))
        flux[0, lev] = flux_x
        flux[1, lev] = flux_y
        col_x += flux_x
        col_y += flux_y
    right, left = lane_shifts(col_x)
    down, up = row_shifts(col_y, 0.0, 0.0)
    top = depth == 0
    source = GRAVITY * (right - left + down - up)
    source = source + jnp.where(top, surface_cot[...], 0.0)
    weight = jnp.where(top, damping[...], 0.0)
    parts = cols // 128
    for h in range(parts):
        lane = slice(128 * h, 128 * (h + 1))
        send[h * rows : (h + 1) * rows] = source[:, lane]
        send[(parts + h) * rows : (parts + h + 1) * rows] = weight[:, lane]
    at = 2 * parts * rows
    kind = lax.broadcasted_iota(jnp.int32, (8, 128), 0)
    ends = jnp.zeros((8, 128), F32)
    for h in range(parts):
        lane = slice(128 * h, 128 * (h + 1))
        ends = jnp.where(kind == h, col_y[0:1, lane], ends)
        ends = jnp.where(kind == parts + h, col_y[rows - 1 : rows, lane], ends)
    send[at : at + 8] = ends

    low_s, high_s = halo(levels * tracers, 8)
    low_s, high_s = ADVECT * GRAVITY * low_s[0:1], ADVECT * GRAVITY * high_s[0:1]
    for j in range(levels):
        lev = level(j, depth, levels)
        at = pl.multiple_of(lev * tracers, tracers)
        low, high = halo(at, tracers)
        first = low_s * packed[2, pl.ds(at, tracers)] + (DIFFUSE - (lines[pl.ds(lev, 1)] + low_s)) * low
        final = high_s * packed[3, pl.ds(at, tracers)] + (DIFFUSE + (lines[pl.ds(levels + lev, 1)] - high_s)) * high
        if j > 0:
            first = first + lines[2 * levels + j - 1 : 2 * levels + j] * delta[0, j - 1]
            final = final + lines[3 * levels + j - 1 : 3 * levels + j] * delta[1, j - 1]
        delta[0, j] = first
        delta[1, j] = final
    at = 2 * parts * rows + 8
    for side in range(2):
        for h in range(parts):
            send[at : at + tracers] = delta[side, levels - 1, :, 128 * h : 128 * (h + 1)]
            at += tracers


def solve_kernel(tiles, partners, flux, mix, nums, last, delta, other_mix, other_last, swept, own, *refs):
    steps = len(partners)
    got, rest = refs[:steps], refs[steps:]
    swaps = sum(differ(pair) for pair in partners)
    swapped, rest = iter(rest[:swaps]), rest[swaps:]
    adj_tracer_out, adj_velocity, adj_surface = rest[:3]
    resid, image, moved, damp, firsts, finals, direc, sol, adj_tracer, sem = rest[3:]
    levels, rows, cols = flux.shape[1:]
    me = lax.axis_index("tile")
    depth = lax.axis_index("depth")

    tracers = last.shape[0]
    inverse, ratio, rest = chain(mix, depth)
    _, _, other_rest = chain(other_mix, 1 - depth)
    own_w, other_w = meet(rest, other_rest, mix[levels - 1], other_mix[levels - 1], depth)
    row = lax.broadcasted_iota(jnp.int32, (rows, cols), 0)
    parts = cols // 128
    far = 2 * parts * rows + 8

    def with_rows(block, first, final):
        return block + (jnp.where(row == 0, first, 0.0) + jnp.where(row == rows - 1, final, 0.0))

    for tr in range(tracers):
        num = with_rows(last[tr], delta[0, levels - 1, tr : tr + 1], delta[1, levels - 1, tr : tr + 1])
        first, final = [
            jnp.concatenate([swept[at + h * tracers : at + h * tracers + 1] for h in range(parts)], axis=1)
            for at in (far + tr, far + parts * tracers + tr)
        ]
        other_num = with_rows(other_last[tr], first, final)
        value = own_w * num + other_w * other_num
        adj_tracer[tr, level(levels - 1, depth, levels)] = value
        for j in range(levels - 2, -1, -1):
            num = with_rows(nums[j, tr], delta[0, j, tr : tr + 1], delta[1, j, tr : tr + 1])
            value = inverse[j] * num + ratio[j] * value
            adj_tracer[tr, level(j, depth, levels)] = value
    copy_out = pltpu.make_async_copy(adj_tracer, adj_tracer_out, sem)
    copy_out.start()

    ends = 2 * parts * rows

    def place(ref, tile):
        for h in range(parts):
            resid[h, pl.ds(tiles + tile, rows, stride=tiles)] = ref[h * rows : (h + 1) * rows]
            damp[h, pl.ds(tile, rows, stride=tiles)] = 4.0 + ref[(parts + h) * rows : (parts + h + 1) * rows]
            firsts[h, pl.ds(tile, 1)] = ref[ends + h : ends + h + 1]
            finals[h, pl.ds(tile, 1)] = ref[ends + parts + h : ends + parts + h + 1]

    place(own, me)
    for step, (for_top, for_bottom) in enumerate(partners):
        place(got[step], partner(me, jnp.where(depth == 0, for_top, for_bottom), tiles))
        if differ((for_top, for_bottom)):
            place(next(swapped), partner(me, jnp.where(depth == 0, for_bottom, for_top), tiles))

    column = lax.broadcasted_iota(jnp.int32, (tiles, 128), 1)

    def group(ref, g):
        return [ref[h, g * tiles : (g + 1) * tiles] for h in range(parts)]

    def keep(ref, g, values):
        for h, value in enumerate(values):
            ref[h, g * tiles : (g + 1) * tiles] = value

    def beside(values):
        left = [pltpu.roll(v, 1, 1) for v in values]
        right = [pltpu.roll(v, 127, 1) for v in values]
        left = [jnp.where(column == 0, left[h - 1] if h > 0 else 0.0, left[h]) for h in range(parts)]
        right = [jnp.where(column == 127, right[h + 1] if h < parts - 1 else 0.0, right[h]) for h in range(parts)]
        return [p + q for p, q in zip(left, right)]

    for h in range(parts):
        next_first, _ = row_shifts(firsts[h], 0.0, 0.0)
        _, last_final = row_shifts(finals[h], 0.0, 0.0)
        resid[h, rows * tiles : (rows + 1) * tiles] += GRAVITY * next_first
        resid[h, tiles : 2 * tiles] -= GRAVITY * last_final

    def sweep(fresh):
        final, first = fresh(rows - 1), fresh(0)
        above = [row_shifts(v, 0.0, 0.0)[1] for v in final]
        after = [row_shifts(v, 0.0, 0.0)[0] for v in first]
        keep(resid, 0, above)
        keep(resid, rows + 1, after)
        norms = [jnp.zeros((tiles, 128), F32)] * parts
        dots = [jnp.zeros((tiles, 128), F32)] * parts
        here = first
        for b in range(rows):
            below = fresh(b + 1) if b + 1 < rows - 1 else final if b + 1 == rows - 1 else after
            side, weight = beside(here), group(damp, b)
            made = [weight[h] * here[h] - ((above[h] + below[h]) + side[h]) for h in range(parts)]
            keep(image, b, made)
            norms = [norms[h] + here[h] * here[h] for h in range(parts)]
            dots = [dots[h] + here[h] * made[h] for h in range(parts)]
            above, here = here, below
        return jnp.sum(sum(norms), keepdims=True), jnp.sum(sum(dots), keepdims=True)

    def step_own(alpha, beta):
        for h in range(parts):
            d = resid[h, pl.ds(me, rows + 2, stride=tiles)] + beta * direc[h]
            direc[h] = d
            sol[h] += alpha * d

    direc[...] = jnp.zeros_like(direc)
    sol[...] = jnp.zeros_like(sol)
    moved[...] = jnp.zeros_like(moved)
    norm, dot = sweep(lambda b: group(resid, b + 1))

    def advance(turn, carry):
        over_norm, inv, alpha, beta = carry
        step_own(alpha, beta)

        def fresh(b):
            old, made, kept = group(resid, b + 1), group(image, b), group(moved, b)
            kept = [made[h] + beta * kept[h] for h in range(parts)]
            new = [old[h] - alpha * kept[h] for h in range(parts)]
            keep(moved, b, kept)
            keep(resid, b + 1, new)
            return new

        norm, dot = sweep(fresh)
        beta = norm * over_norm
        divisor = dot - norm * (beta * inv)
        over_norm = 1.0 / norm
        return over_norm, divisor * over_norm, norm / divisor, beta

    over_norm = 1.0 / norm
    first = (over_norm, dot * over_norm, norm / dot, jnp.zeros_like(norm))
    _, _, alpha, beta = lax.fori_loop(0, ITERS - 1, advance, first)
    step_own(alpha, beta)

    x = jnp.concatenate([sol[h, 1 : rows + 1] for h in range(parts)], axis=1)
    adj_surface[...] = x
    right, left = lane_shifts(x)
    slope_x = ADVECT * (right - left)
    slope_y = jnp.concatenate([ADVECT * (sol[h, 2 : rows + 2] - sol[h, 0:rows]) for h in range(parts)], axis=1)
    for lev in range(levels):
        adj_velocity[0, lev] = flux[0, lev] + slope_x
        adj_velocity[1, lev] = flux[1, lev] + slope_y
    copy_out.wait()


def solve_call(partners, args, tiles):
    flux, last = args[0], args[3]
    tracers = last.shape[0]
    levels, rows, cols = flux.shape[1:]
    plane, height, parts = (rows, cols), tiles * rows, cols // 128
    block = (tracers, levels) + plane
    return call(
        functools.partial(solve_kernel, tiles, partners),
        [block, (2, levels) + plane, plane],
        args,
        scratch=[
            pltpu.VMEM((parts, height + 2 * tiles, 128), F32),
            pltpu.VMEM((parts, height, 128), F32),
            pltpu.VMEM((parts, height, 128), F32),
            pltpu.VMEM((parts, height, 128), F32),
            pltpu.VMEM((parts, tiles, 128), F32),
            pltpu.VMEM((parts, tiles, 128), F32),
            pltpu.VMEM((parts, rows + 2, 128), F32),
            pltpu.VMEM((parts, rows + 2, 128), F32),
            pltpu.VMEM(block, F32),
            pltpu.SemaphoreType.DMA(()),
        ],
        hbm_out=(0,),
    )


def partner(tile, offset, tiles):
    if tiles & (tiles - 1) == 0:
        return tile ^ offset
    return (offset + tiles - tile) % tiles


def differ(pair):
    return pair[0] != pair[1]


def partner_offsets(tiles):
    if tiles & (tiles - 1) == 0:
        others = sorted(range(1, tiles), key=lambda k: (bin(k).count("1"), k))
    else:
        others = list(range(tiles))
    if len(others) % 2 == 1:
        others = others[:1] + others
    return [(others[i], others[i + 1]) for i in range(0, len(others), 2)]


def body(tracer_start, velocity, surface, mixing, land_mask, damping, tracer_cot, surface_cot):
    tracers, levels, rows, cols = tracer_start.shape
    tiles = lax.axis_size("tile")
    swap = [(0, 1), (1, 0)]
    plane = (rows, cols)
    block = (tracers, levels) + plane
    edge = (tracers * levels + 8, cols)
    edge_b, edge_a = call(
        edge_kernel,
        [edge, edge],
        [tracer_cot.reshape(tracers * levels, rows, cols), land_mask, surface, tracer_start, mixing, velocity],
        scratch=[
            pltpu.VMEM((2, tracers * levels, 8, cols), F32),
            pltpu.VMEM((2, levels, 8, cols), jnp.int32),
            pltpu.VMEM((2, 8, cols), F32),
            pltpu.SemaphoreType.DMA((6,)),
        ],
        hbm_in=range(6),
        near=True,
    )
    pairs_a = [(i, i + 1) for i in range(0, tiles - 1, 2)]
    pairs_b = [(i, i + 1) for i in range(1, tiles - 1, 2)]
    other = lax.ppermute(tracer_start, "depth", swap)
    other_mix = lax.ppermute(mixing, "depth", swap)
    edge_b = lax.ppermute(edge_b, "tile", pairs_b + [(b, a) for a, b in pairs_b])
    edge_a = lax.ppermute(edge_a, "tile", pairs_a + [(b, a) for a, b in pairs_a])
    planes, parts = tracers * levels, cols // 128
    share = 2 * parts * rows + 8
    flux, nums, last, packed, lines = call(
        interior_kernel,
        [(2, levels) + plane, (levels - 1, tracers) + plane, (tracers,) + plane, (4, planes, cols), (4 * levels, cols)],
        [tracer_start, mixing, tracer_cot, land_mask, velocity, surface, other, other_mix],
        scratch=[pltpu.VMEM((2, levels) + plane, F32)],
    )
    flux, delta, part = call(
        column_kernel,
        [(2, levels) + plane, (2, levels, tracers, cols), (share + 2 * parts * tracers, 128)],
        [flux, packed, lines, edge_b, edge_a, surface_cot, damping],
    )
    swept = lax.ppermute(part, "depth", swap)
    own = part[:share] + swept[:share]

    partners = partner_offsets(tiles)
    got = []
    for for_top, for_bottom in partners:
        pairs = [(2 * partner(t, for_top, tiles), 2 * t) for t in range(tiles)]
        pairs += [(2 * partner(t, for_bottom, tiles) + 1, 2 * t + 1) for t in range(tiles)]
        got.append(lax.ppermute(own, ("tile", "depth"), pairs))
    swapped = [lax.ppermute(piece, "depth", swap) for piece, pair in zip(got, partners) if differ(pair)]

    other_last = lax.ppermute(last, "depth", swap)
    return solve_call(
        partners,
        [flux, mixing, nums, last, delta, other_mix, other_last, swept, own] + got + swapped,
        tiles,
    )


def solution(mesh):
    return jax.shard_map(
        body,
        mesh=mesh,
        in_specs=(
            P("grp", "depth", "tile", None),
            P("grp", "depth", "tile", None),
            P(("grp", "tile"), None),
            P(("grp", "depth"), "tile", None),
            P("depth", "tile", None),
            P("tile", None),
            P("grp", "depth", "tile", None),
            P(("grp", "tile"), None),
        ),
        out_specs=(
            P("grp", "depth", "tile", None),
            P("grp", "depth", "tile", None),
            P(("grp", "tile"), None),
        ),
        check_vma=False,
    )
```
